256 devices in a mesh: pipe: 16 (over y, z_lo), fsdp: 16 (over z_hi, x, core).
Axes of the slice: x: 4, y: 4, z: 8 (z_hi: 2, z_lo: 4; z = z_hi * 4 + z_lo), core: 2. Of those that a mesh axis runs over, the one named last changes fastest.
Arguments:
- latents: bfloat16 [4, 512, 6144], P(None, 'fsdp'), may hold values from -6 to 6
- upstream: bfloat16 [4, 512, 6144], P(None, 'fsdp'), may hold values from -0.1875 to 0.1875
- proj_in: bfloat16 [16, 6144, 256], P('pipe', 'fsdp'), may hold values from -0.078125 to 0.078125
- proj_out: bfloat16 [16, 256, 6144], P('pipe', None, 'fsdp'), may hold values from -0.375 to 0.375
- norm_gain: float32 [16, 6144], P('pipe'), may hold values from 0.1 to 1.9
Outputs:
- grad_in: bfloat16 [16, 6144, 256], P('pipe', 'fsdp')
- grad_out: bfloat16 [16, 256, 6144], P('pipe', None, 'fsdp')
The draws below stay inside these ranges and needn't reach their ends.
All inputs are finite; a program needn't handle non-finite values.
Results may differ from the reference program's by a relative error of at most 0.035.
Values may be sent and summed in bfloat16 or wider, within the bound.
A program may use at most 64 MiB of HBM per device.

```python
import jax
import jax.numpy as jnp
from jax import lax

D = 6144
R = 256
M = 4
ROWS = 32
TOKENS = 512
SECTIONS = 16
N_FSDP = 16


def with_spikes(drawn, own_key, source, target, shards_of, factor):
    def block_of(dim):
        return (jnp.arange(drawn.shape[dim]) // (drawn.shape[dim] // shards_of)).reshape((-1,) + (1,) * (drawn.ndim - 1 - dim))

    one_side = jax.random.permutation(own_key, shards_of)[block_of(target)]
    other_side = (block_of(target) + shards_of // 2) % shards_of
    return jnp.where((block_of(source) == one_side) | (block_of(source) == other_side), factor * drawn, drawn)


def block_scale(key, shape, cuts, smallest, largest):
    gain, own = 1.0, jax.random.fold_in(key, 6)
    for position, shards_of in cuts:
        draws = jnp.exp(jax.random.uniform(jax.random.fold_in(own, position), (shards_of,), jnp.float32, smallest / len(cuts), largest / len(cuts)))
        gain = gain * jnp.repeat(draws, shape[position] // shards_of).reshape([-1 if axis == position else 1 for axis in range(len(shape))])
    return gain


def centred(stream_key, dims, spread, bound, split=(), kind=jnp.bfloat16):
    gain = block_scale(stream_key, dims, split, -0.22, 0.18) if split else 1.0
    values = jax.random.normal(stream_key, dims, jnp.float32) * spread * gain
    return jnp.minimum(jnp.maximum(values, -bound), bound).astype(kind)


def heavy_noise(own_key, dims, deviation, limit, shards, heavy, dtype=jnp.bfloat16):
    array = deviation * jax.random.normal(own_key, dims, jnp.float32)
    if shards:
        array = array * block_scale(own_key, dims, shards, -0.22, 0.18)
    return jnp.clip(with_spikes(array, jax.random.fold_in(own_key, 3), *heavy), -limit, limit).astype(dtype)


def setup_inputs(seed: int = 0) -> dict:
    streams_of = jax.random.split(jax.random.key(seed), 6)
    return {
        "latents": centred(streams_of[0], (M, TOKENS, D), 1.0, 6.0, ((1, 16),)),
        "upstream": heavy_noise(streams_of[1], (M, TOKENS, D), (M * TOKENS) ** -0.5, 0.1875, ((1, 16),), (1, 2, 16, 2.0)),
        "proj_in": centred(streams_of[2], (SECTIONS, D, R), D ** -0.5, 0.078125, ((0, 16), (1, 16))),
        "proj_out": centred(streams_of[3], (SECTIONS, R, D), R ** -0.5, 0.375, ((0, 16), (2, 16))),
        "norm_gain": jnp.clip(1.0 + 0.18 * jax.random.normal(streams_of[4], (SECTIONS, D), jnp.float32), 0.1, 1.9),
    }


epsilon = 1e-06
root_half = 0.7071067811865476
inv_root_tau = 0.3989422804014327

def gelu_pair(preact):
    normal_cdf = 0.5 * (1.0 + lax.erf(preact * root_half))
    return (preact * normal_cdf, normal_cdf + preact * jnp.exp(-0.5 * preact * preact) * inv_root_tau)

def normalize(hidden, gain_row):
    hidden_f32 = hidden.astype(jnp.float32)
    inverse = lax.rsqrt(lax.optimization_barrier(jnp.mean(hidden_f32 * hidden_f32, axis=-1, keepdims=True)) + epsilon)
    scaled = hidden_f32 * inverse
    return (hidden_f32, inverse, scaled, (scaled * gain_row).astype(jnp.bfloat16))

def forward_rows(hidden, weight_in, weight_out, gain_row):
    hidden_f32, inverse, scaled, normed = normalize(hidden, gain_row)
    preact = jnp.dot(normed, weight_in, preferred_element_type=jnp.float32)
    activated = gelu_pair(preact)[0].astype(jnp.bfloat16)
    branch = jnp.dot(activated, weight_out, preferred_element_type=jnp.float32)
    return (hidden_f32 + branch).astype(jnp.bfloat16)

def backward_rows(hidden, grad_next, weight_in, weight_out, gain_row):
    hidden_f32, inverse, scaled, normed = normalize(hidden, gain_row)
    preact = jnp.dot(normed, weight_in, preferred_element_type=jnp.float32)
    gelu_result, derivative = gelu_pair(preact)
    activated = gelu_result.astype(jnp.bfloat16)
    grad_act = jnp.dot(grad_next, weight_out.T, preferred_element_type=jnp.float32)
    grad_pre = (grad_act * derivative).astype(jnp.bfloat16)
    grad_normed = jnp.dot(grad_pre, weight_in.T, preferred_element_type=jnp.float32)
    grad_scaled = grad_normed * gain_row
    grad_path = inverse * (grad_scaled - scaled * lax.optimization_barrier(jnp.mean(grad_scaled * scaled, axis=-1, keepdims=True)))
    grad_here = (grad_next.astype(jnp.float32) + grad_path).astype(jnp.bfloat16)
    return (grad_here, normed, activated, grad_pre)

def reference(latents, upstream, proj_in, proj_out, norm_gain):

    def one_group(group_index, totals):
        row_start = (group_index * ROWS).astype(jnp.int32)
        rows_in = lax.dynamic_slice_in_dim(latents, row_start, ROWS, 1).reshape(M * ROWS, D)
        grads_top = lax.dynamic_slice_in_dim(upstream, row_start, ROWS, 1).reshape(M * ROWS, D)

        def forward_step(hidden, params):
            weight_in, weight_out, gain_row = params
            return (forward_rows(hidden, weight_in, weight_out, gain_row), hidden)
        _, stash = lax.scan(forward_step, rows_in, (proj_in, proj_out, norm_gain))

        def backward_step(grad_next, params):
            weight_in, weight_out, gain_row, hidden = params
            grad_here, normed, activated, grad_pre = backward_rows(hidden, grad_next, weight_in, weight_out, gain_row)
            part_in = jnp.dot(normed.T, grad_pre, preferred_element_type=jnp.float32).astype(jnp.bfloat16)
            part_out = jnp.dot(activated.T, grad_next, preferred_element_type=jnp.float32).astype(jnp.bfloat16)
            return (grad_here, (part_in, part_out))
        _, parts = lax.scan(backward_step, grads_top, (proj_in, proj_out, norm_gain, stash), reverse=True)
        parts_in, parts_out = lax.optimization_barrier(parts)
        return (totals[0] + parts_in.astype(jnp.float32), totals[1] + parts_out.astype(jnp.float32))
    start_in = jnp.zeros((SECTIONS, D, R), jnp.float32)
    start_out = jnp.zeros((SECTIONS, R, D), jnp.float32)
    totals = lax.fori_loop(0, N_FSDP, one_group, (start_in, start_out))
    return (totals[0].astype(jnp.bfloat16), totals[1].astype(jnp.bfloat16))
```

```python
import functools

import jax
import jax.numpy as jnp
from jax import lax
from jax.experimental import pallas as pl
from jax.experimental.pallas import tpu as pltpu
from jax.sharding import PartitionSpec as P

MESH = pl.DeviceIdType.MESH
epsilon = 1e-06
root_half = 0.7071067811865476
inv_root_tau = 0.3989422804014327
ROWS = 16
CHUNKS = 3


def relay_kernel(
    stages, blocks, features,
    lat_ref, up_ref, win_ref, wout_ref, pin_ref, pout_ref,
    h_in, h_out, g_in, g_out, act_s, slope_s, pre_s, inv_s, q_s,
    f_send, f_recv, b_send, b_recv,
):
    s = lax.axis_index("pipe")
    f = lax.axis_index("fsdp")
    wide = features // CHUNKS
    after = lax.rem(s + 1, stages)
    before = lax.rem(s + stages - 1, stages)

    barrier = pltpu.get_barrier_semaphore()
    for other in (before, after):
        pl.semaphore_signal(barrier, inc=1, device_id=(other, f), device_id_type=MESH)
    pl.semaphore_wait(barrier, 2)

    def columns(c):
        return pl.ds(c * wide, wide)

    def f_copy(i, c):
        return pltpu.make_async_remote_copy(
            src_ref=h_out.at[i, :, columns(c)], dst_ref=h_in.at[i, :, columns(c)],
            send_sem=f_send.at[i, c], recv_sem=f_recv.at[i, c],
            device_id=(after, f), device_id_type=MESH,
        )

    def b_copy(i, c):
        return pltpu.make_async_remote_copy(
            src_ref=g_out.at[i, :, columns(c)], dst_ref=g_in.at[i, :, columns(c)],
            send_sem=b_send.at[i, c], recv_sem=b_recv.at[i, c],
            device_id=(before, f), device_id_type=MESH,
        )

    @pl.when(s == 0)
    def _():
        @pl.loop(0, blocks)
        def _(i):
            for c in range(CHUNKS):
                pltpu.make_async_copy(
                    lat_ref.at[i, :, columns(c)], h_in.at[i, :, columns(c)], f_recv.at[i, c]
                ).start()

    @pl.when(s == stages - 1)
    def _():
        @pl.loop(0, blocks)
        def _(i):
            for c in range(CHUNKS):
                pltpu.make_async_copy(
                    up_ref.at[i, :, columns(c)], g_in.at[i, :, columns(c)], b_recv.at[i, c]
                ).start()

    def forward(i):
        pre = jnp.zeros((ROWS, win_ref.shape[1]), jnp.float32)
        square = jnp.zeros((ROWS, 1), jnp.float32)
        for c in range(CHUNKS):
            f_copy(i, c).wait_recv()
            h = h_in[i, :, columns(c)]
            pre += jnp.dot(h, win_ref[columns(c), :], preferred_element_type=jnp.float32)
            wide_h = h.astype(jnp.float32)
            square += jnp.sum(wide_h * wide_h, axis=-1, keepdims=True)
        inverse = lax.rsqrt(square * (1.0 / features) + epsilon)
        pre = pre * inverse
        cdf = 0.5 * (1.0 + lax.erf(pre * root_half))
        act = (pre * cdf).astype(jnp.bfloat16)

        @pl.when(s < stages - 1)
        def _():
            for c in range(CHUNKS):
                branch = jnp.dot(act, wout_ref[:, columns(c)], preferred_element_type=jnp.float32)
                h_out[i, :, columns(c)] = (
                    h_in[i, :, columns(c)].astype(jnp.float32) + branch
                ).astype(jnp.bfloat16)
                f_copy(i, c).start()

        act_s[i] = act
        pre_s[i] = pre
        slope_s[i] = cdf + pre * jnp.exp(-0.5 * pre * pre) * inv_root_tau
        inv_s[i] = jnp.broadcast_to(inverse, pre.shape)

    def backward(i):
        grad_act = jnp.zeros((ROWS, win_ref.shape[1]), jnp.float32)
        for c in range(CHUNKS):
            b_copy(i, c).wait_recv()
            grad_act += lax.dot_general(
                g_in[i, :, columns(c)], wout_ref[:, columns(c)], (((1,), (1,)), ((), ())),
                preferred_element_type=jnp.float32,
            )
        grad_pre = grad_act * slope_s[i]
        inverse = inv_s[i]
        mean = jnp.sum(grad_pre * pre_s[i], axis=-1, keepdims=True) * (1.0 / features)
        q = (grad_pre * inverse).astype(jnp.bfloat16)
        q_s[i] = q
        pull = inverse[:, :1] * inverse[:, :1] * mean

        @pl.when(s > 0)
        def _():
            for c in range(CHUNKS):
                path = lax.dot_general(
                    q, win_ref[columns(c), :], (((1,), (1,)), ((), ())),
                    preferred_element_type=jnp.float32,
                )
                g_out[i, :, columns(c)] = (
                    g_in[i, :, columns(c)].astype(jnp.float32) + path
                    - pull * h_in[i, :, columns(c)].astype(jnp.float32)
                ).astype(jnp.bfloat16)
                b_copy(i, c).start()

    @pl.loop(0, blocks + 2 * stages - 2)
    def _(tick):
        ahead = tick - s
        back = tick - (2 * stages - 2) + s

        @pl.when((ahead >= 0) & (ahead < blocks))
        def _():
            forward(ahead)

        @pl.when((back >= 0) & (back < blocks))
        def _():
            backward(back)

    tokens = blocks * ROWS
    part = 512
    q_all = q_s[...].reshape(tokens, -1)
    act_all = act_s[...].reshape(tokens, -1)

    @pl.loop(0, features // part)
    def _(n):
        cut = pl.ds(pl.multiple_of(n * part, part), part)
        h = h_in[:, :, cut].reshape(tokens, part)
        pin_ref[cut, :] = lax.dot_general(
            h, q_all, (((0,), (0,)), ((), ())), preferred_element_type=jnp.float32
        ).astype(jnp.bfloat16)
        g = g_in[:, :, cut].reshape(tokens, part)
        pout_ref[:, cut] = lax.dot_general(
            act_all, g, (((0,), (0,)), ((), ())), preferred_element_type=jnp.float32
        ).astype(jnp.bfloat16)

    @pl.when(s < stages - 1)
    def _():
        @pl.loop(0, blocks)
        def _(i):
            for c in range(CHUNKS):
                f_copy(i, c).wait_send()

    @pl.when(s > 0)
    def _():
        @pl.loop(0, blocks)
        def _(i):
            for c in range(CHUNKS):
                b_copy(i, c).wait_send()


def per_device(latents, upstream, proj_in, proj_out, norm_gain):
    stages = lax.axis_size("pipe")
    shards = lax.axis_size("fsdp")
    f = lax.axis_index("fsdp")
    features = latents.shape[2]
    inner = proj_in.shape[2]
    share = features // shards
    gain = lax.dynamic_slice_in_dim(norm_gain[0], f * share, share)[:, None]
    scaled_in = (proj_in[0].astype(jnp.float32) * gain).astype(jnp.bfloat16)
    weight_in = lax.all_gather(scaled_in, "fsdp", axis=0, tiled=True)
    weight_out = lax.all_gather(proj_out[0], "fsdp", axis=1, tiled=True)
    blocks = latents.shape[0] * latents.shape[1] // ROWS
    lat = latents.reshape(blocks, ROWS, features)
    up = upstream.reshape(blocks, ROWS, features)
    vmem = pl.BlockSpec(memory_space=pltpu.VMEM)
    anywhere = pl.BlockSpec(memory_space=pl.ANY)
    wide_buffer = pltpu.VMEM((blocks, ROWS, features), jnp.bfloat16)
    narrow = pltpu.VMEM((blocks, ROWS, inner), jnp.bfloat16)
    narrow_f32 = pltpu.VMEM((blocks, ROWS, inner), jnp.float32)
    sems = pltpu.SemaphoreType.DMA((blocks, CHUNKS))
    part_in, part_out = pl.pallas_call(
        functools.partial(relay_kernel, stages, blocks, features),
        out_shape=(
            jax.ShapeDtypeStruct((features, inner), jnp.bfloat16),
            jax.ShapeDtypeStruct((inner, features), jnp.bfloat16),
        ),
        in_specs=[anywhere, anywhere, vmem, vmem],
        out_specs=(vmem, vmem),
        scratch_shapes=[
            wide_buffer, wide_buffer, wide_buffer, wide_buffer,
            narrow, narrow_f32, narrow_f32, narrow_f32, narrow,
            sems, sems, sems, sems,
        ],
        compiler_params=pltpu.CompilerParams(
            collective_id=0, has_side_effects=True, vmem_limit_bytes=48 * 1024 * 1024
        ),
        name="relay",
    )(lat, up, weight_in, weight_out)
    grad_in = lax.psum_scatter(part_in, "fsdp", scatter_dimension=0, tiled=True)
    grad_out = lax.psum_scatter(part_out, "fsdp", scatter_dimension=1, tiled=True)
    grad_in = (grad_in.astype(jnp.float32) * gain).astype(jnp.bfloat16)
    return grad_in[None], grad_out[None]


def solution(mesh):
    in_specs = (
        P(None, "fsdp", None),
        P(None, "fsdp", None),
        P("pipe", "fsdp", None),
        P("pipe", None, "fsdp"),
        P("pipe", None),
    )
    out_specs = (P("pipe", "fsdp", None), P("pipe", None, "fsdp"))
    return jax.shard_map(
        per_device, mesh=mesh, in_specs=in_specs, out_specs=out_specs, check_vma=False
    )
```

```python
import functools

import jax
import jax.numpy as jnp
from jax import lax
from jax.experimental import pallas as pl
from jax.experimental.pallas import tpu as pltpu
from jax.sharding import PartitionSpec as P

MESH = pl.DeviceIdType.MESH
epsilon = 1e-06
root_half = 0.7071067811865476
inv_root_tau = 0.3989422804014327
ROWS = 16
CHUNKS = 3


def relay_kernel(
    stages, blocks, features,
    lat_ref, up_ref, pin_ref, pout_ref, gain_ref, gin_ref, gout_ref,
    win_ref, wout_ref,
    h_in, h_out, g_in, g_out, act_s, slope_s, pre_s, inv_s, q_s,
    pair_in, pair_out, pair_in_stage, pair_out_stage,
    ring_in, ring_out, ring_in_stage, ring_out_stage,
    far_in, far_out, far_in_stage, far_out_stage, sum_in, sum_out,
    f_send, f_recv, b_send, b_recv, ag_send, ag_recv,
    pair_send, pair_recv, ring_send, ring_recv, far_send, far_recv,
):
    s = lax.axis_index("pipe")
    f = lax.axis_index("fsdp")
    wide = features // CHUNKS
    share = pin_ref.shape[0]
    after = lax.rem(s + 1, stages)
    before = lax.rem(s + stages - 1, stages)
    half = f // 8
    place = lax.rem(f, 8) // 2
    core = lax.rem(f, 2)

    def index_of(z, x, c):
        return z * 8 + lax.rem(x + 4, 4) * 2 + c

    right = index_of(half, place + 1, core)
    left = index_of(half, place - 1, core)
    pair = index_of(half, place, 1 - core)
    far = index_of(1 - half, place, core)

    barrier = pltpu.get_barrier_semaphore()
    for other in ((before, f), (after, f), (s, right), (s, left), (s, pair), (s, far)):
        pl.semaphore_signal(barrier, inc=1, device_id=other, device_id_type=MESH)

    def rows_of(j):
        return pl.ds(pl.multiple_of(j * share, 128), share)

    win_ref[rows_of(f), :] = (pin_ref[...].astype(jnp.float32) * gain_ref[...]).astype(jnp.bfloat16)
    wout_ref[:, rows_of(f)] = pout_ref[...]
    pl.semaphore_wait(barrier, 6)

    routes = (far, right, left, pair)

    def shard(j, piece):
        return win_ref.at[rows_of(j), :] if piece == 0 else wout_ref.at[:, rows_of(j)]

    def spread(j, piece, route):
        return pltpu.make_async_remote_copy(
            src_ref=shard(j, piece), dst_ref=shard(j, piece),
            send_sem=ag_send.at[route, j, piece], recv_sem=ag_recv.at[j, piece],
            device_id=(s, routes[route]), device_id_type=MESH,
        )

    sent = []

    def share_out(j, piece, *ways):
        for way in ways:
            spread(j, piece, way).start()
            sent.append((j, piece, way))

    def arrived(j, piece):
        spread(j, piece, 3).wait_recv()

    for piece in (0, 1):
        share_out(f, piece, 0)
    for piece in (0, 1):
        share_out(f, piece, 1, 2)
    for piece in (0, 1):
        share_out(f, piece, 3)

    def columns(c):
        return pl.ds(c * wide, wide)

    def f_copy(i, c):
        return pltpu.make_async_remote_copy(
            src_ref=h_out.at[i, :, columns(c)], dst_ref=h_in.at[i, :, columns(c)],
            send_sem=f_send.at[i, c], recv_sem=f_recv.at[i, c],
            device_id=(after, f), device_id_type=MESH,
        )

    def b_copy(i, c):
        return pltpu.make_async_remote_copy(
            src_ref=g_out.at[i, :, columns(c)], dst_ref=g_in.at[i, :, columns(c)],
            send_sem=b_send.at[i, c], recv_sem=b_recv.at[i, c],
            device_id=(before, f), device_id_type=MESH,
        )

    @pl.when(s == 0)
    def _():
        @pl.loop(0, blocks)
        def _(i):
            for c in range(CHUNKS):
                pltpu.make_async_copy(
                    lat_ref.at[i, :, columns(c)], h_in.at[i, :, columns(c)], f_recv.at[i, c]
                ).start()

    @pl.when(s == stages - 1)
    def _():
        @pl.loop(0, blocks)
        def _(i):
            for c in range(CHUNKS):
                pltpu.make_async_copy(
                    up_ref.at[i, :, columns(c)], g_in.at[i, :, columns(c)], b_recv.at[i, c]
                ).start()

    for z in (half, 1 - half):
        mine, on_left, on_right, across = [index_of(z, place + step, core) for step in (0, -1, 1, 2)]
        if z is not half:
            for piece in (0, 1):
                arrived(mine, piece)
                share_out(mine, piece, 1, 2, 3)
        arrived(on_left, 0)
        share_out(on_left, 0, 1, 3)
        arrived(on_right, 0)
        share_out(on_right, 0, 3)
        arrived(on_right, 1)
        share_out(on_right, 1, 2, 3)
        arrived(on_left, 1)
        share_out(on_left, 1, 3)
        for piece in (0, 1):
            arrived(across, piece)
            share_out(across, piece, 3)
    for z in (half, 1 - half):
        for step in (0, -1, 1, 2):
            for piece in (0, 1):
                arrived(index_of(z, place + step, 1 - core), piece)
    def forward(i):
        pre = jnp.zeros((ROWS, win_ref.shape[1]), jnp.float32)
        square = jnp.zeros((ROWS, 1), jnp.float32)
        for c in range(CHUNKS):
            f_copy(i, c).wait_recv()
            h = h_in[i, :, columns(c)]
            pre += jnp.dot(h, win_ref[columns(c), :], preferred_element_type=jnp.float32)
            wide_h = h.astype(jnp.float32)
            square += jnp.sum(wide_h * wide_h, axis=-1, keepdims=True)
        inverse = lax.rsqrt(square * (1.0 / features) + epsilon)
        pre = pre * inverse
        cdf = 0.5 * (1.0 + lax.erf(pre * root_half))
        act = (pre * cdf).astype(jnp.bfloat16)

        @pl.when(s < stages - 1)
        def _():
            for c in range(CHUNKS):
                branch = jnp.dot(act, wout_ref[:, columns(c)], preferred_element_type=jnp.float32)
                h_out[i, :, columns(c)] = (
                    h_in[i, :, columns(c)].astype(jnp.float32) + branch
                ).astype(jnp.bfloat16)
                f_copy(i, c).start()

        act_s[i] = act
        pre_s[i] = pre
        slope_s[i] = cdf + pre * jnp.exp(-0.5 * pre * pre) * inv_root_tau
        inv_s[i] = jnp.broadcast_to(inverse, pre.shape)

    def backward(i):
        grad_act = jnp.zeros((ROWS, win_ref.shape[1]), jnp.float32)
        for c in range(CHUNKS):
            b_copy(i, c).wait_recv()
            grad_act += lax.dot_general(
                g_in[i, :, columns(c)], wout_ref[:, columns(c)], (((1,), (1,)), ((), ())),
                preferred_element_type=jnp.float32,
            )
        grad_pre = grad_act * slope_s[i]
        inverse = inv_s[i]
        mean = jnp.sum(grad_pre * pre_s[i], axis=-1, keepdims=True) * (1.0 / features)
        q = (grad_pre * inverse).astype(jnp.bfloat16)
        q_s[i] = q
        pull = inverse[:, :1] * inverse[:, :1] * mean

        @pl.when(s > 0)
        def _():
            for c in range(CHUNKS):
                path = lax.dot_general(
                    q, win_ref[columns(c), :], (((1,), (1,)), ((), ())),
                    preferred_element_type=jnp.float32,
                )
                g_out[i, :, columns(c)] = (
                    g_in[i, :, columns(c)].astype(jnp.float32) + path
                    - pull * h_in[i, :, columns(c)].astype(jnp.float32)
                ).astype(jnp.bfloat16)
                b_copy(i, c).start()

    @pl.loop(0, blocks + 2 * stages - 2)
    def _(tick):
        ahead = tick - s
        back = tick - (2 * stages - 2) + s

        @pl.when((ahead >= 0) & (ahead < blocks))
        def _():
            forward(ahead)

        @pl.when((back >= 0) & (back < blocks))
        def _():
            backward(back)

    tokens = blocks * ROWS
    q_all = q_s[...].reshape(tokens, -1)
    act_all = act_s[...].reshape(tokens, -1)
    over_tokens = (((0,), (0,)), ((), ()))

    def part_in(j):
        h = h_in[:, :, rows_of(j)].reshape(tokens, share)
        return lax.dot_general(h, q_all, over_tokens, preferred_element_type=jnp.float32)

    def part_out(j):
        g = g_in[:, :, rows_of(j)].reshape(tokens, share)
        return lax.dot_general(act_all, g, over_tokens, preferred_element_type=jnp.float32)

    def remote(src, dst, send, recv, route):
        return pltpu.make_async_remote_copy(
            src_ref=src, dst_ref=dst, send_sem=send, recv_sem=recv,
            device_id=(s, routes[route]), device_id_type=MESH,
        )

    def pair_copy(m, piece):
        stage, land = ((pair_in_stage, pair_in), (pair_out_stage, pair_out))[piece]
        return remote(stage.at[m], land.at[m], pair_send.at[m, piece], pair_recv.at[m, piece], 3)

    def ring_copy(h, slot, piece):
        stage, land = ((ring_in_stage, ring_in), (ring_out_stage, ring_out))[piece]
        way = 1 if (slot == 2) == (piece == 1) else 2
        return remote(
            stage.at[h, slot], land.at[h, slot],
            ring_send.at[h, slot, piece], ring_recv.at[h, slot, piece], way,
        )

    def far_copy(piece):
        stage, land = ((far_in_stage, far_in), (far_out_stage, far_out))[piece]
        return remote(stage, land, far_send.at[piece], far_recv.at[piece], 0)

    steps = (2, 1, -1, 0)
    halves = (1 - half, half)
    for h in (0, 1):
        for k, step in enumerate(steps):
            m = h * 4 + k
            j = index_of(halves[h], place + step, 1 - core)
            pair_in_stage[m] = part_in(j).astype(jnp.bfloat16)
            pair_copy(m, 0).start()
            pair_out_stage[m] = part_out(j).astype(jnp.bfloat16)
            pair_copy(m, 1).start()

    def both_in(h, k):
        pair_copy(h * 4 + k, 0).wait_recv()
        j = index_of(halves[h], place + steps[k], core)
        return part_in(j) + pair_in[h * 4 + k].astype(jnp.float32)

    def both_out(h, k):
        pair_copy(h * 4 + k, 1).wait_recv()
        j = index_of(halves[h], place + steps[k], core)
        return part_out(j) + pair_out[h * 4 + k].astype(jnp.float32)

    for h in (0, 1):
        ring_in_stage[h, 0] = both_in(h, 0).astype(jnp.bfloat16)
        ring_copy(h, 0, 0).start()
        ring_out_stage[h, 0] = both_out(h, 0).astype(jnp.bfloat16)
        ring_copy(h, 0, 1).start()
        ring_out_stage[h, 2] = both_out(h, 1).astype(jnp.bfloat16)
        ring_copy(h, 2, 1).start()
        ring_in_stage[h, 2] = both_in(h, 2).astype(jnp.bfloat16)
        ring_copy(h, 2, 0).start()
        sum_in[h] = both_in(h, 3)
        sum_out[h] = both_out(h, 3)
    for h in (0, 1):
        own = both_in(h, 1)
        ring_copy(h, 0, 0).wait_recv()
        ring_in_stage[h, 1] = (own + ring_in[h, 0].astype(jnp.float32)).astype(jnp.bfloat16)
        ring_copy(h, 1, 0).start()
        own = both_out(h, 2)
        ring_copy(h, 0, 1).wait_recv()
        ring_out_stage[h, 1] = (own + ring_out[h, 0].astype(jnp.float32)).astype(jnp.bfloat16)
        ring_copy(h, 1, 1).start()

    def total(h, piece):
        kept, land = ((sum_in, ring_in), (sum_out, ring_out))[piece]
        for slot in (2, 1):
            ring_copy(h, slot, piece).wait_recv()
        return kept[h] + land[h, 1].astype(jnp.float32) + land[h, 2].astype(jnp.float32)

    far_in_stage[...] = total(0, 0).astype(jnp.bfloat16)
    far_copy(0).start()
    far_out_stage[...] = total(0, 1).astype(jnp.bfloat16)
    far_copy(1).start()
    own = total(1, 0)
    far_copy(0).wait_recv()
    gin_ref[...] = ((own + far_in[...].astype(jnp.float32)) * gain_ref[...]).astype(jnp.bfloat16)
    own = total(1, 1)
    far_copy(1).wait_recv()
    gout_ref[...] = (own + far_out[...].astype(jnp.float32)).astype(jnp.bfloat16)

    for j, piece, way in sent:
        spread(j, piece, way).wait_send()
    for piece in (0, 1):
        far_copy(piece).wait_send()
        for m in range(8):
            pair_copy(m, piece).wait_send()
        for h in (0, 1):
            for slot in range(3):
                ring_copy(h, slot, piece).wait_send()

    @pl.when(s < stages - 1)
    def _():
        @pl.loop(0, blocks)
        def _(i):
            for c in range(CHUNKS):
                f_copy(i, c).wait_send()

    @pl.when(s > 0)
    def _():
        @pl.loop(0, blocks)
        def _(i):
            for c in range(CHUNKS):
                b_copy(i, c).wait_send()


def per_device(latents, upstream, proj_in, proj_out, norm_gain):
    stages = lax.axis_size("pipe")
    shards = lax.axis_size("fsdp")
    f = lax.axis_index("fsdp")
    features = latents.shape[2]
    inner = proj_in.shape[2]
    share = features // shards
    gain = lax.dynamic_slice_in_dim(norm_gain[0], f * share, share)[:, None]
    blocks = latents.shape[0] * latents.shape[1] // ROWS
    lat = latents.reshape(blocks, ROWS, features)
    up = upstream.reshape(blocks, ROWS, features)
    vmem = pl.BlockSpec(memory_space=pltpu.VMEM)
    anywhere = pl.BlockSpec(memory_space=pl.ANY)

    def low(*shape):
        return pltpu.VMEM(shape, jnp.bfloat16)

    def high(*shape):
        return pltpu.VMEM(shape, jnp.float32)

    def sems(*shape):
        return pltpu.SemaphoreType.DMA(shape)

    tall, flat = (share, inner), (inner, share)
    grad_in, grad_out = pl.pallas_call(
        functools.partial(relay_kernel, stages, blocks, features),
        out_shape=(
            jax.ShapeDtypeStruct(tall, jnp.bfloat16),
            jax.ShapeDtypeStruct(flat, jnp.bfloat16),
        ),
        in_specs=[anywhere, anywhere, vmem, vmem, vmem],
        out_specs=(vmem, vmem),
        scratch_shapes=[
            low(features, inner), low(inner, features),
            *[low(blocks, ROWS, features)] * 4,
            low(blocks, ROWS, inner), *[high(blocks, ROWS, inner)] * 3, low(blocks, ROWS, inner),
            low(8, *tall), low(8, *flat), low(8, *tall), low(8, *flat),
            low(2, 3, *tall), low(2, 3, *flat), low(2, 3, *tall), low(2, 3, *flat),
            low(*tall), low(*flat), low(*tall), low(*flat), high(2, *tall), high(2, *flat),
            *[sems(blocks, CHUNKS)] * 4, sems(4, shards, 2), sems(shards, 2),
            sems(8, 2), sems(8, 2), sems(2, 3, 2), sems(2, 3, 2), sems(2), sems(2),
        ],
        compiler_params=pltpu.CompilerParams(
            collective_id=0, has_side_effects=True, vmem_limit_bytes=48 * 1024 * 1024
        ),
        name="relay",
    )(lat, up, proj_in[0], proj_out[0], gain)
    return grad_in[None], grad_out[None]


def solution(mesh):
    in_specs = (
        P(None, "fsdp", None),
        P(None, "fsdp", None),
        P("pipe", "fsdp", None),
        P("pipe", None, "fsdp"),
        P("pipe", None),
    )
    out_specs = (P("pipe", "fsdp", None), P("pipe", None, "fsdp"))
    return jax.shard_map(
        per_device, mesh=mesh, in_specs=in_specs, out_specs=out_specs, check_vma=False
    )
```

```python
import functools

import jax
import jax.numpy as jnp
from jax import lax
from jax.experimental import pallas as pl
from jax.experimental.pallas import tpu as pltpu
from jax.sharding import PartitionSpec as P

MESH = pl.DeviceIdType.MESH
epsilon = 1e-06
root_half = 0.7071067811865476
inv_root_tau = 0.3989422804014327
TOKENS = 8
ROWS = 16
CHUNKS = 3
LAG = 2


def relay_kernel(
    stages, blocks, features,
    lat_ref, up_ref, pin_ref, pout_ref, gain_ref, gin_ref, gout_ref,
    win_ref, wout_ref, win_t, wout_t, own_in, own_gain, gain_s, top,
    h_in, h_out, g_in, g_out, slope_s, pre_s, inv_s, act_s, q_s,
    pair_in, pair_out, pair_in_stage, pair_out_stage,
    ring_in, ring_out, ring_in_stage, ring_out_stage,
    far_in, far_out, far_in_stage, far_out_stage, sum_in, sum_out,
    load_sem, top_sem, f_send, f_recv, b_send, b_recv, ag_send, ag_recv,
    pair_send, pair_recv, ring_send, ring_recv, far_send, far_recv,
):
    s = lax.axis_index("pipe")
    f = lax.axis_index("fsdp")
    fold = features // 2
    wide = fold // CHUNKS
    inner = pin_ref.shape[1]
    share = pin_ref.shape[0]
    after = lax.rem(s + 1, stages)
    before = lax.rem(s + stages - 1, stages)
    half = f // 8
    place = lax.rem(f, 8) // 2
    core = lax.rem(f, 2)

    def index_of(z, x, c):
        return z * 8 + lax.rem(x + 4, 4) * 2 + c

    right = index_of(half, place + 1, core)
    left = index_of(half, place - 1, core)
    pair = index_of(half, place, 1 - core)
    far = index_of(1 - half, place, core)

    def rows_of(j):
        return pl.ds(pl.multiple_of(j * share, 128), share)

    loads = (
        pltpu.make_async_copy(gain_ref.at[:, rows_of(f)], own_gain, load_sem.at[0]),
        pltpu.make_async_copy(pin_ref, own_in, load_sem.at[1]),
        pltpu.make_async_copy(pout_ref, wout_ref.at[:, rows_of(f)], load_sem.at[2]),
    )
    for load in loads:
        load.start()

    barrier = pltpu.get_barrier_semaphore()
    for other in ((before, f), (after, f), (s, right), (s, left), (s, pair), (s, far)):
        pl.semaphore_signal(barrier, inc=1, device_id=other, device_id_type=MESH)

    for load in loads:
        load.wait()
    gain_s[...] = jnp.broadcast_to(own_gain[...], (128, share)).T

    def gains():
        return jnp.concatenate([gain_s[...]] * (inner // 128), axis=1)

    win_ref[rows_of(f), :] = (own_in[...].astype(jnp.float32) * gains()).astype(jnp.bfloat16)
    pl.semaphore_wait(barrier, 6)

    routes = (far, right, left, pair)

    def shard(j, piece):
        return win_ref.at[rows_of(j), :] if piece == 0 else wout_ref.at[:, rows_of(j)]

    def spread(j, piece, route):
        return pltpu.make_async_remote_copy(
            src_ref=shard(j, piece), dst_ref=shard(j, piece),
            send_sem=ag_send.at[route, j, piece], recv_sem=ag_recv.at[j, piece],
            device_id=(s, routes[route]), device_id_type=MESH,
        )

    sent = []

    def share_out(j, piece, *ways):
        for way in ways:
            spread(j, piece, way).start()
            sent.append((j, piece, way))

    def arrived(j, piece):
        spread(j, piece, 3).wait_recv()

    def reach_far(turn):
        @pl.when(lax.rem(s, 4) == turn)
        def _():
            for piece in (0, 1):
                spread(f, piece, 0).start()

    for piece in (0, 1):
        sent.append((f, piece, 0))
    reach_far(0)
    for piece in (0, 1):
        share_out(f, piece, 1, 2)
    for piece in (0, 1):
        share_out(f, piece, 3)

    def columns(c):
        return pl.ds(c * wide, wide)

    def f_copy(i, c):
        return pltpu.make_async_remote_copy(
            src_ref=h_out.at[i, :, columns(c)], dst_ref=h_in.at[i, :, columns(c)],
            send_sem=f_send.at[i, c], recv_sem=f_recv.at[i, c],
            device_id=(after, f), device_id_type=MESH,
        )

    def b_copy(i, c):
        return pltpu.make_async_remote_copy(
            src_ref=g_out.at[i, :, columns(c)], dst_ref=g_in.at[i, :, columns(c)],
            send_sem=b_send.at[i, c], recv_sem=b_recv.at[i, c],
            device_id=(before, f), device_id_type=MESH,
        )

    def folded(upper, lower):
        return jnp.concatenate([upper, lower], axis=0)

    def load_folded(source, target, land, sem):
        load = pltpu.make_async_copy(source, top, top_sem)
        load.start()
        load.wait()

        @pl.loop(0, blocks // 2)
        def _(i):
            for c in range(CHUNKS):
                low = top[i, :, columns(c)].astype(jnp.float32)
                high = top[i, :, pl.ds(fold + c * wide, wide)].astype(jnp.float32)
                for k in (0, 1):
                    rows = slice(k * TOKENS, (k + 1) * TOKENS)
                    target[2 * i + k, :, columns(c)] = folded(low[rows], high[rows]).astype(jnp.bfloat16)
                    pltpu.make_async_copy(
                        target.at[2 * i + k, :, columns(c)], land.at[2 * i + k, :, columns(c)],
                        sem.at[2 * i + k, c],
                    ).start()

    @pl.when(s == 0)
    def _():
        load_folded(lat_ref, g_out, h_in, f_recv)

    @pl.when(s == stages - 1)
    def _():
        load_folded(up_ref, h_out, g_in, b_recv)

    for z in (half, 1 - half):
        mine, on_left, on_right, across = [index_of(z, place + step, core) for step in (0, -1, 1, 2)]
        if z is not half:
            for piece in (0, 1):
                arrived(mine, piece)
                share_out(mine, piece, 1, 2, 3)
        arrived(on_left, 0)
        share_out(on_left, 0, 1, 3)
        if z is half:
            reach_far(1)
        arrived(on_right, 0)
        share_out(on_right, 0, 3)
        arrived(on_right, 1)
        share_out(on_right, 1, 2, 3)
        arrived(on_left, 1)
        share_out(on_left, 1, 3)
        if z is half:
            reach_far(2)
        for piece in (0, 1):
            arrived(across, piece)
            share_out(across, piece, 3)
        if z is half:
            reach_far(3)
    for z in (half, 1 - half):
        for step in (0, -1, 1, 2):
            for piece in (0, 1):
                arrived(index_of(z, place + step, 1 - core), piece)
    def transpose_weights():
        @pl.loop(0, features // 512)
        def _(n):
            cut = pl.ds(pl.multiple_of(n * 512, 512), 512)
            wout_t[cut, :] = wout_ref[:, cut].T
            win_t[:, cut] = win_ref[cut, :].T

    def forward(i):
        low = jnp.zeros((ROWS, inner), jnp.float32)
        high = jnp.zeros((ROWS, inner), jnp.float32)
        square = jnp.zeros((ROWS, 1), jnp.float32)
        for c in range(CHUNKS):
            f_copy(i, c).wait_recv()
            h = h_in[i, :, columns(c)]
            low += jnp.dot(h, win_ref[columns(c), :], preferred_element_type=jnp.float32)
            high += jnp.dot(
                h, win_ref[pl.ds(fold + c * wide, wide), :], preferred_element_type=jnp.float32
            )
            wide_h = h.astype(jnp.float32)
            square += jnp.sum(wide_h * wide_h, axis=-1, keepdims=True)
        square = square[:TOKENS] + square[TOKENS:]
        inverse = lax.rsqrt(square * (1.0 / features) + epsilon)
        pre = (low[:TOKENS] + high[TOKENS:]) * inverse
        cdf = 0.5 * (1.0 + lax.erf(pre * root_half))
        act = pre * cdf

        @pl.when(s < stages - 1)
        def _():
            both = folded(act, act).astype(jnp.bfloat16)
            for c in range(CHUNKS):
                upper = jnp.dot(both, wout_ref[:, columns(c)], preferred_element_type=jnp.float32)
                lower = jnp.dot(
                    both, wout_ref[:, pl.ds(fold + c * wide, wide)],
                    preferred_element_type=jnp.float32,
                )
                h_out[i, :, columns(c)] = (
                    h_in[i, :, columns(c)].astype(jnp.float32)
                    + folded(upper[:TOKENS], lower[TOKENS:])
                ).astype(jnp.bfloat16)
                f_copy(i, c).start()

        blank = jnp.zeros_like(act)
        act_s[0, i] = folded(act, blank).astype(jnp.bfloat16)
        act_s[1, i] = folded(blank, act).astype(jnp.bfloat16)
        pre_s[i] = pre
        slope_s[i] = cdf + pre * jnp.exp(-0.5 * pre * pre) * inv_root_tau
        inv_s[i] = jnp.broadcast_to(inverse, pre.shape)

    def backward(i):
        low = jnp.zeros((ROWS, inner), jnp.float32)
        high = jnp.zeros((ROWS, inner), jnp.float32)
        for c in range(CHUNKS):
            b_copy(i, c).wait_recv()
            g = g_in[i, :, columns(c)]
            low += jnp.dot(g, wout_t[columns(c), :], preferred_element_type=jnp.float32)
            high += jnp.dot(
                g, wout_t[pl.ds(fold + c * wide, wide), :], preferred_element_type=jnp.float32
            )
        grad_pre = (low[:TOKENS] + high[TOKENS:]) * slope_s[i]
        inverse = inv_s[i]
        mean = jnp.sum(grad_pre * pre_s[i], axis=-1, keepdims=True) * (1.0 / features)
        q = grad_pre * inverse
        pull = inverse[:, :1] * inverse[:, :1] * mean

        @pl.when(s > 0)
        def _():
            both = folded(q, q).astype(jnp.bfloat16)
            pulls = folded(pull, pull)
            for c in range(CHUNKS):
                upper = jnp.dot(both, win_t[:, columns(c)], preferred_element_type=jnp.float32)
                lower = jnp.dot(
                    both, win_t[:, pl.ds(fold + c * wide, wide)],
                    preferred_element_type=jnp.float32,
                )
                g_out[i, :, columns(c)] = (
                    g_in[i, :, columns(c)].astype(jnp.float32)
                    + folded(upper[:TOKENS], lower[TOKENS:])
                    - pulls * h_in[i, :, columns(c)].astype(jnp.float32)
                ).astype(jnp.bfloat16)
                b_copy(i, c).start()

        blank = jnp.zeros_like(q)
        q_s[0, i] = folded(q, blank).astype(jnp.bfloat16)
        q_s[1, i] = folded(blank, q).astype(jnp.bfloat16)

    @pl.when(s >= 4)
    def _():
        transpose_weights()

    @pl.loop(0, blocks + LAG * (2 * stages - 2))
    def _(tick):
        @pl.when((s < 4) & (tick == LAG * s + blocks))
        def _():
            transpose_weights()

        ahead = tick - LAG * s
        back = tick - LAG * (2 * stages - 2 - s)

        @pl.when((ahead >= 0) & (ahead < blocks))
        def _():
            forward(ahead)

        @pl.when((back >= 0) & (back < blocks))
        def _():
            backward(back)

    rows = blocks * ROWS
    over_rows = (((0,), (0,)), ((), ()))

    def cut_of(j):
        return pl.ds(pl.multiple_of(lax.rem(j, 8) * share, 128), share)

    def part_in(j):
        h = h_in[:, :, cut_of(j)].reshape(rows, share)
        q = q_s[j // 8].reshape(rows, inner)
        return lax.dot_general(h, q, over_rows, preferred_element_type=jnp.float32)

    def part_out(j):
        g = g_in[:, :, cut_of(j)].reshape(rows, share)
        act = act_s[j // 8].reshape(rows, inner)
        return lax.dot_general(act, g, over_rows, preferred_element_type=jnp.float32)

    def remote(src, dst, send, recv, route):
        return pltpu.make_async_remote_copy(
            src_ref=src, dst_ref=dst, send_sem=send, recv_sem=recv,
            device_id=(s, routes[route]), device_id_type=MESH,
        )

    def pair_copy(m, piece):
        stage, land = ((pair_in_stage, pair_in), (pair_out_stage, pair_out))[piece]
        return remote(stage.at[m], land.at[m], pair_send.at[m, piece], pair_recv.at[m, piece], 3)

    def ring_copy(h, slot, piece):
        stage, land = ((ring_in_stage, ring_in), (ring_out_stage, ring_out))[piece]
        way = 1 if (slot == 2) == (piece == 1) else 2
        return remote(
            stage.at[h, slot], land.at[h, slot],
            ring_send.at[h, slot, piece], ring_recv.at[h, slot, piece], way,
        )

    def far_copy(piece):
        stage, land = ((far_in_stage, far_in), (far_out_stage, far_out))[piece]
        return remote(stage, land, far_send.at[piece], far_recv.at[piece], 0)

    steps = (2, 1, -1, 0)
    halves = (1 - half, half)
    def pair_share(h):
        for k, step in enumerate(steps):
            m = h * 4 + k
            j = index_of(halves[h], place + step, 1 - core)
            pair_in_stage[m] = part_in(j).astype(jnp.bfloat16)
            pair_copy(m, 0).start()
            pair_out_stage[m] = part_out(j).astype(jnp.bfloat16)
            pair_copy(m, 1).start()

    def both_in(h, k):
        pair_copy(h * 4 + k, 0).wait_recv()
        j = index_of(halves[h], place + steps[k], core)
        return part_in(j) + pair_in[h * 4 + k].astype(jnp.float32)

    def both_out(h, k):
        pair_copy(h * 4 + k, 1).wait_recv()
        j = index_of(halves[h], place + steps[k], core)
        return part_out(j) + pair_out[h * 4 + k].astype(jnp.float32)

    def open_ring(h):
        ring_in_stage[h, 0] = both_in(h, 0).astype(jnp.bfloat16)
        ring_copy(h, 0, 0).start()
        ring_out_stage[h, 0] = both_out(h, 0).astype(jnp.bfloat16)
        ring_copy(h, 0, 1).start()
        ring_out_stage[h, 2] = both_out(h, 1).astype(jnp.bfloat16)
        ring_copy(h, 2, 1).start()
        ring_in_stage[h, 2] = both_in(h, 2).astype(jnp.bfloat16)
        ring_copy(h, 2, 0).start()
        sum_in[h] = both_in(h, 3)
        sum_out[h] = both_out(h, 3)

    def relay_ring(h):
        own = both_in(h, 1)
        ring_copy(h, 0, 0).wait_recv()
        ring_in_stage[h, 1] = (own + ring_in[h, 0].astype(jnp.float32)).astype(jnp.bfloat16)
        ring_copy(h, 1, 0).start()
        own = both_out(h, 2)
        ring_copy(h, 0, 1).wait_recv()
        ring_out_stage[h, 1] = (own + ring_out[h, 0].astype(jnp.float32)).astype(jnp.bfloat16)
        ring_copy(h, 1, 1).start()

    def total(h, piece):
        kept, land = ((sum_in, ring_in), (sum_out, ring_out))[piece]
        for slot in (2, 1):
            ring_copy(h, slot, piece).wait_recv()
        return kept[h] + land[h, 1].astype(jnp.float32) + land[h, 2].astype(jnp.float32)

    pair_share(0)
    open_ring(0)
    pair_share(1)
    relay_ring(0)
    open_ring(1)
    far_in_stage[...] = total(0, 0).astype(jnp.bfloat16)
    far_copy(0).start()
    far_out_stage[...] = total(0, 1).astype(jnp.bfloat16)
    far_copy(1).start()
    relay_ring(1)
    own = total(1, 0)
    far_copy(0).wait_recv()
    gin_ref[...] = ((own + far_in[...].astype(jnp.float32)) * gains()).astype(jnp.bfloat16)
    own = total(1, 1)
    far_copy(1).wait_recv()
    gout_ref[...] = (own + far_out[...].astype(jnp.float32)).astype(jnp.bfloat16)

    for j, piece, way in sent:
        spread(j, piece, way).wait_send()
    for piece in (0, 1):
        far_copy(piece).wait_send()
        for m in range(8):
            pair_copy(m, piece).wait_send()
        for h in (0, 1):
            for slot in range(3):
                ring_copy(h, slot, piece).wait_send()

    @pl.when(s < stages - 1)
    def _():
        @pl.loop(0, blocks)
        def _(i):
            for c in range(CHUNKS):
                f_copy(i, c).wait_send()

    @pl.when(s > 0)
    def _():
        @pl.loop(0, blocks)
        def _(i):
            for c in range(CHUNKS):
                b_copy(i, c).wait_send()


def per_device(latents, upstream, proj_in, proj_out, norm_gain):
    stages = lax.axis_size("pipe")
    shards = lax.axis_size("fsdp")
    features = latents.shape[2]
    inner = proj_in.shape[2]
    share = features // shards
    blocks = latents.shape[0] * latents.shape[1] // TOKENS
    lat = latents.reshape(blocks // 2, ROWS, features)
    up = upstream.reshape(blocks // 2, ROWS, features)
    vmem = pl.BlockSpec(memory_space=pltpu.VMEM)
    anywhere = pl.BlockSpec(memory_space=pltpu.HBM)

    def low(*shape):
        return pltpu.VMEM(shape, jnp.bfloat16)

    def high(*shape):
        return pltpu.VMEM(shape, jnp.float32)

    def sems(*shape):
        return pltpu.SemaphoreType.DMA(shape)

    tall, flat = (share, inner), (inner, share)
    grad_in, grad_out = pl.pallas_call(
        functools.partial(relay_kernel, stages, blocks, features),
        out_shape=(
            jax.ShapeDtypeStruct(tall, jnp.bfloat16),
            jax.ShapeDtypeStruct(flat, jnp.bfloat16),
        ),
        in_specs=[anywhere] * 5,
        out_specs=(vmem, vmem),
        scratch_shapes=[
            low(features, inner), low(inner, features), low(inner, features), low(features, inner),
            low(*tall), high(1, share), high(share, 128),
            low(blocks // 2, ROWS, features), *[low(blocks, ROWS, features // 2)] * 4,
            *[high(blocks, TOKENS, inner)] * 3, *[low(2, blocks, ROWS, inner)] * 2,
            low(8, *tall), low(8, *flat), low(8, *tall), low(8, *flat),
            low(2, 3, *tall), low(2, 3, *flat), low(2, 3, *tall), low(2, 3, *flat),
            low(*tall), low(*flat), low(*tall), low(*flat), high(2, *tall), high(2, *flat),
            sems(3), pltpu.SemaphoreType.DMA, *[sems(blocks, CHUNKS)] * 4, sems(4, shards, 2), sems(shards, 2),
            sems(8, 2), sems(8, 2), sems(2, 3, 2), sems(2, 3, 2), sems(2), sems(2),
        ],
        compiler_params=pltpu.CompilerParams(
            collective_id=0, has_side_effects=True, vmem_limit_bytes=48 * 1024 * 1024
        ),
        name="relay",
    )(lat, up, proj_in[0], proj_out[0], norm_gain)
    return grad_in[None], grad_out[None]


def solution(mesh):
    in_specs = (
        P(None, "fsdp", None),
        P(None, "fsdp", None),
        P("pipe", "fsdp", None),
        P("pipe", None, "fsdp"),
        P("pipe", None),
    )
    out_specs = (P("pipe", "fsdp", None), P("pipe", None, "fsdp"))
    return jax.shard_map(
        per_device, mesh=mesh, in_specs=in_specs, out_specs=out_specs, check_vma=False
    )
```

```python
import functools

import jax
import jax.numpy as jnp
from jax import lax
from jax.experimental import pallas as pl
from jax.experimental.pallas import tpu as pltpu
from jax.sharding import PartitionSpec as P

MESH = pl.DeviceIdType.MESH
epsilon = 1e-06
root_half = 0.7071067811865476
inv_root_tau = 0.3989422804014327
TOKENS = 8
ROWS = 16
CHUNKS = 3
LAG = 2
VMEM_BYTES = 64 * 1024 * 1024 - 65536


def relay_kernel(
    stages, blocks, features,
    lat_ref, up_ref, pin_ref, pout_ref, gain_ref, gin_ref, gout_ref,
    win_ref, wout_ref, win_t, wout_t, own_in, own_gain, gain_s, top,
    h_in, h_out, g_in, g_out, slope_s, pre_s, inv_s, act_s, q_s,
    pair_in, pair_out, pair_in_stage, pair_out_stage,
    ring_in, ring_out, ring_in_stage, ring_out_stage,
    far_in, far_out, far_in_stage, far_out_stage, sum_in, sum_out,
    load_sem, top_sem, f_send, f_recv, b_send, b_recv, ag_send, ag_recv,
    pair_send, pair_recv, ring_send, ring_recv, far_send, far_recv, turn,
):
    s = lax.axis_index("pipe")
    f = lax.axis_index("fsdp")
    fold = features // 2
    wide = fold // CHUNKS
    inner = pin_ref.shape[1]
    share = pin_ref.shape[0]
    after = lax.rem(s + 1, stages)
    before = lax.rem(s + stages - 1, stages)
    half = f // 8
    place = lax.rem(f, 8) // 2
    core = lax.rem(f, 2)

    def index_of(z, x, c):
        return z * 8 + lax.rem(x + 4, 4) * 2 + c

    right = index_of(half, place + 1, core)
    left = index_of(half, place - 1, core)
    pair = index_of(half, place, 1 - core)
    far = index_of(1 - half, place, core)

    def rows_of(j):
        return pl.ds(pl.multiple_of(j * share, 128), share)

    loads = (
        pltpu.make_async_copy(gain_ref.at[:, rows_of(f)], own_gain, load_sem.at[0]),
        pltpu.make_async_copy(pin_ref, own_in, load_sem.at[1]),
        pltpu.make_async_copy(pout_ref, wout_ref.at[:, rows_of(f)], load_sem.at[2]),
    )
    for load in loads:
        load.start()

    barrier = pltpu.get_barrier_semaphore()
    for other in ((before, f), (after, f), (s, right), (s, left), (s, pair), (s, far)):
        pl.semaphore_signal(barrier, inc=1, device_id=other, device_id_type=MESH)

    for load in loads:
        load.wait()
    gain_s[...] = jnp.broadcast_to(own_gain[...], (128, share)).T

    def gains():
        return jnp.concatenate([gain_s[...]] * (inner // 128), axis=1)

    win_ref[rows_of(f), :] = (own_in[...].astype(jnp.float32) * gains()).astype(jnp.bfloat16)
    def columns(c):
        return pl.ds(c * wide, wide)

    def folded(upper, lower):
        return jnp.concatenate([upper, lower], axis=0)

    def load_folded(source, target, land, sem):
        load = pltpu.make_async_copy(source, top, top_sem)
        load.start()
        load.wait()

        @pl.loop(0, blocks // 2)
        def _(i):
            for c in range(CHUNKS):
                low = top[i, :, columns(c)].astype(jnp.float32)
                high = top[i, :, pl.ds(fold + c * wide, wide)].astype(jnp.float32)
                for k in (0, 1):
                    rows = slice(k * TOKENS, (k + 1) * TOKENS)
                    target[2 * i + k, :, columns(c)] = folded(low[rows], high[rows]).astype(jnp.bfloat16)
                    pltpu.make_async_copy(
                        target.at[2 * i + k, :, columns(c)], land.at[2 * i + k, :, columns(c)],
                        sem.at[2 * i + k, c],
                    ).start()

    @pl.when(s == 0)
    def _():
        load_folded(lat_ref, g_out, h_in, f_recv)

    @pl.when(s == stages - 1)
    def _():
        load_folded(up_ref, h_out, g_in, b_recv)

    pl.semaphore_wait(barrier, 6)

    routes = (far, right, left, pair)

    def shard(j, piece):
        return win_ref.at[rows_of(j), :] if piece == 0 else wout_ref.at[:, rows_of(j)]

    def spread(j, piece, route):
        return pltpu.make_async_remote_copy(
            src_ref=shard(j, piece), dst_ref=shard(j, piece),
            send_sem=ag_send.at[route, j, piece], recv_sem=ag_recv.at[j, piece],
            device_id=(s, routes[route]), device_id_type=MESH,
        )

    sent = []

    def share_out(j, piece, *ways):
        for way in ways:
            spread(j, piece, way).start()
            sent.append((j, piece, way))

    def arrived(j, piece):
        spread(j, piece, 3).wait_recv()

    def reach_far(turn):
        @pl.when(lax.rem(s, 4) == turn)
        def _():
            for piece in (0, 1):
                spread(f, piece, 0).start()

    for piece in (0, 1):
        sent.append((f, piece, 0))
    reach_far(0)
    for piece in (0, 1):
        share_out(f, piece, 1, 2)
    for piece in (0, 1):
        share_out(f, piece, 3)

    def f_copy(i, c):
        return pltpu.make_async_remote_copy(
            src_ref=h_out.at[i, :, columns(c)], dst_ref=h_in.at[i, :, columns(c)],
            send_sem=f_send.at[i, c], recv_sem=f_recv.at[i, c],
            device_id=(after, f), device_id_type=MESH,
        )

    def b_copy(i, c):
        return pltpu.make_async_remote_copy(
            src_ref=g_out.at[i, :, columns(c)], dst_ref=g_in.at[i, :, columns(c)],
            send_sem=b_send.at[i, c], recv_sem=b_recv.at[i, c],
            device_id=(before, f), device_id_type=MESH,
        )

    for z in (half, 1 - half):
        mine, on_left, on_right, across = [index_of(z, place + step, core) for step in (0, -1, 1, 2)]
        if z is not half:
            for piece in (0, 1):
                arrived(mine, piece)
                share_out(mine, piece, 1, 2, 3)
        arrived(on_left, 0)
        share_out(on_left, 0, 1, 3)
        if z is half:
            reach_far(1)
        arrived(on_right, 0)
        share_out(on_right, 0, 3)
        arrived(on_right, 1)
        share_out(on_right, 1, 2, 3)
        arrived(on_left, 1)
        share_out(on_left, 1, 3)
        if z is half:
            reach_far(2)
        for piece in (0, 1):
            arrived(across, piece)
            share_out(across, piece, 3)
        if z is half:
            reach_far(3)
    for z in (half, 1 - half):
        for step in (0, -1, 1, 2):
            for piece in (0, 1):
                arrived(index_of(z, place + step, 1 - core), piece)
    def transpose_weights():
        @pl.loop(0, features // 512)
        def _(n):
            cut = pl.ds(pl.multiple_of(n * 512, 512), 512)
            wout_t[cut, :] = wout_ref[:, cut].T
            win_t[:, cut] = win_ref[cut, :].T

    def forward(i):
        low = jnp.zeros((ROWS, inner), jnp.float32)
        high = jnp.zeros((ROWS, inner), jnp.float32)
        square = jnp.zeros((ROWS, 1), jnp.float32)
        for c in range(CHUNKS):
            f_copy(i, c).wait_recv()
            h = h_in[i, :, columns(c)]
            low += jnp.dot(h, win_ref[columns(c), :], preferred_element_type=jnp.float32)
            high += jnp.dot(
                h, win_ref[pl.ds(fold + c * wide, wide), :], preferred_element_type=jnp.float32
            )
            wide_h = h.astype(jnp.float32)
            square += jnp.sum(wide_h * wide_h, axis=-1, keepdims=True)
        square = square[:TOKENS] + square[TOKENS:]
        inverse = lax.rsqrt(square * (1.0 / features) + epsilon)
        pre = (low[:TOKENS] + high[TOKENS:]) * inverse
        cdf = 0.5 * (1.0 + lax.erf(pre * root_half))
        act = pre * cdf

        @pl.when(s < stages - 1)
        def _():
            both = folded(act, act).astype(jnp.bfloat16)
            for c in range(CHUNKS):
                upper = jnp.dot(both, wout_ref[:, columns(c)], preferred_element_type=jnp.float32)
                lower = jnp.dot(
                    both, wout_ref[:, pl.ds(fold + c * wide, wide)],
                    preferred_element_type=jnp.float32,
                )
                h_out[i, :, columns(c)] = (
                    h_in[i, :, columns(c)].astype(jnp.float32)
                    + folded(upper[:TOKENS], lower[TOKENS:])
                ).astype(jnp.bfloat16)
                f_copy(i, c).start()

        blank = jnp.zeros_like(act)
        act_s[0, i] = folded(act, blank).astype(jnp.bfloat16)
        act_s[1, i] = folded(blank, act).astype(jnp.bfloat16)
        pre_s[i] = pre
        slope_s[i] = cdf + pre * jnp.exp(-0.5 * pre * pre) * inv_root_tau
        inv_s[i] = jnp.broadcast_to(inverse, pre.shape)

    def backward(i):
        low = jnp.zeros((ROWS, inner), jnp.float32)
        high = jnp.zeros((ROWS, inner), jnp.float32)
        for c in range(CHUNKS):
            b_copy(i, c).wait_recv()
            g = g_in[i, :, columns(c)]
            low += jnp.dot(g, wout_t[columns(c), :], preferred_element_type=jnp.float32)
            high += jnp.dot(
                g, wout_t[pl.ds(fold + c * wide, wide), :], preferred_element_type=jnp.float32
            )
        grad_pre = (low[:TOKENS] + high[TOKENS:]) * slope_s[i]
        inverse = inv_s[i]
        mean = jnp.sum(grad_pre * pre_s[i], axis=-1, keepdims=True) * (1.0 / features)
        q = grad_pre * inverse
        pull = inverse[:, :1] * inverse[:, :1] * mean

        @pl.when(s > 0)
        def _():
            both = folded(q, q).astype(jnp.bfloat16)
            pulls = folded(pull, pull)
            for c in range(CHUNKS):
                upper = jnp.dot(both, win_t[:, columns(c)], preferred_element_type=jnp.float32)
                lower = jnp.dot(
                    both, win_t[:, pl.ds(fold + c * wide, wide)],
                    preferred_element_type=jnp.float32,
                )
                g_out[i, :, columns(c)] = (
                    g_in[i, :, columns(c)].astype(jnp.float32)
                    + folded(upper[:TOKENS], lower[TOKENS:])
                    - pulls * h_in[i, :, columns(c)].astype(jnp.float32)
                ).astype(jnp.bfloat16)
                b_copy(i, c).start()

        blank = jnp.zeros_like(q)
        q_s[0, i] = folded(q, blank).astype(jnp.bfloat16)
        q_s[1, i] = folded(blank, q).astype(jnp.bfloat16)

    @pl.when(s >= 4)
    def _():
        transpose_weights()

    @pl.loop(0, blocks + LAG * (2 * stages - 2))
    def _(tick):
        @pl.when((s < 4) & (tick == LAG * s + blocks))
        def _():
            transpose_weights()

        ahead = tick - LAG * s
        back = tick - LAG * (2 * stages - 2 - s)

        @pl.when((ahead >= 0) & (ahead < blocks))
        def _():
            @pl.when((s == 0) & (core == 1) & (ahead == 0))
            def _():
                pl.semaphore_wait(turn, 1)

            forward(ahead)

            @pl.when((s == 0) & (core == 0) & (ahead == 0))
            def _():
                pl.semaphore_signal(turn, inc=1, device_id=(s, pair), device_id_type=MESH)

        @pl.when((back >= 0) & (back < blocks))
        def _():
            backward(back)

    rows = blocks * ROWS
    over_rows = (((0,), (0,)), ((), ()))

    def cut_of(j):
        return pl.ds(pl.multiple_of(lax.rem(j, 8) * share, 128), share)

    def part_in(j):
        h = h_in[:, :, cut_of(j)].reshape(rows, share)
        q = q_s[j // 8].reshape(rows, inner)
        return lax.dot_general(h, q, over_rows, preferred_element_type=jnp.float32)

    def part_out(j):
        g = g_in[:, :, cut_of(j)].reshape(rows, share)
        act = act_s[j // 8].reshape(rows, inner)
        return lax.dot_general(act, g, over_rows, preferred_element_type=jnp.float32)

    def remote(src, dst, send, recv, route):
        return pltpu.make_async_remote_copy(
            src_ref=src, dst_ref=dst, send_sem=send, recv_sem=recv,
            device_id=(s, routes[route]), device_id_type=MESH,
        )

    def pair_copy(m, piece):
        stage, land = ((pair_in_stage, pair_in), (pair_out_stage, pair_out))[piece]
        return remote(stage.at[m], land.at[m], pair_send.at[m, piece], pair_recv.at[m, piece], 3)

    def ring_copy(h, slot, piece):
        stage, land = ((ring_in_stage, ring_in), (ring_out_stage, ring_out))[piece]
        way = 1 if (slot == 2) == (piece == 1) else 2
        return remote(
            stage.at[h, slot], land.at[h, slot],
            ring_send.at[h, slot, piece], ring_recv.at[h, slot, piece], way,
        )

    def far_copy(piece):
        stage, land = ((far_in_stage, far_in), (far_out_stage, far_out))[piece]
        return remote(stage, land, far_send.at[piece], far_recv.at[piece], 0)

    steps = (2, 1, -1, 0)
    halves = (1 - half, half)
    def pair_share(h):
        for k, step in enumerate(steps):
            m = h * 4 + k
            j = index_of(halves[h], place + step, 1 - core)
            pair_in_stage[m] = part_in(j).astype(jnp.bfloat16)
            pair_copy(m, 0).start()
            pair_out_stage[m] = part_out(j).astype(jnp.bfloat16)
            pair_copy(m, 1).start()

    def both_in(h, k):
        pair_copy(h * 4 + k, 0).wait_recv()
        j = index_of(halves[h], place + steps[k], core)
        return part_in(j) + pair_in[h * 4 + k].astype(jnp.float32)

    def both_out(h, k):
        pair_copy(h * 4 + k, 1).wait_recv()
        j = index_of(halves[h], place + steps[k], core)
        return part_out(j) + pair_out[h * 4 + k].astype(jnp.float32)

    def open_ring(h):
        ring_in_stage[h, 0] = both_in(h, 0).astype(jnp.bfloat16)
        ring_copy(h, 0, 0).start()
        ring_out_stage[h, 0] = both_out(h, 0).astype(jnp.bfloat16)
        ring_copy(h, 0, 1).start()
        ring_out_stage[h, 2] = both_out(h, 1).astype(jnp.bfloat16)
        ring_copy(h, 2, 1).start()
        ring_in_stage[h, 2] = both_in(h, 2).astype(jnp.bfloat16)
        ring_copy(h, 2, 0).start()
        sum_in[h] = both_in(h, 3)
        sum_out[h] = both_out(h, 3)

    def relay_ring(h):
        own = both_in(h, 1)
        ring_copy(h, 0, 0).wait_recv()
        ring_in_stage[h, 1] = (own + ring_in[h, 0].astype(jnp.float32)).astype(jnp.bfloat16)
        ring_copy(h, 1, 0).start()
        own = both_out(h, 2)
        ring_copy(h, 0, 1).wait_recv()
        ring_out_stage[h, 1] = (own + ring_out[h, 0].astype(jnp.float32)).astype(jnp.bfloat16)
        ring_copy(h, 1, 1).start()

    def total(h, piece):
        kept, land = ((sum_in, ring_in), (sum_out, ring_out))[piece]
        for slot in (2, 1):
            ring_copy(h, slot, piece).wait_recv()
        return kept[h] + land[h, 1].astype(jnp.float32) + land[h, 2].astype(jnp.float32)

    pair_share(0)
    open_ring(0)
    pair_share(1)
    relay_ring(0)
    open_ring(1)
    far_in_stage[...] = total(0, 0).astype(jnp.bfloat16)
    far_copy(0).start()
    far_out_stage[...] = total(0, 1).astype(jnp.bfloat16)
    far_copy(1).start()
    relay_ring(1)
    own = total(1, 0)
    far_copy(0).wait_recv()
    gin_ref[...] = ((own + far_in[...].astype(jnp.float32)) * gains()).astype(jnp.bfloat16)
    own = total(1, 1)
    far_copy(1).wait_recv()
    gout_ref[...] = (own + far_out[...].astype(jnp.float32)).astype(jnp.bfloat16)

    for j, piece, way in sent:
        spread(j, piece, way).wait_send()
    for piece in (0, 1):
        far_copy(piece).wait_send()
        for m in range(8):
            pair_copy(m, piece).wait_send()
        for h in (0, 1):
            for slot in range(3):
                ring_copy(h, slot, piece).wait_send()

    @pl.when(s < stages - 1)
    def _():
        @pl.loop(0, blocks)
        def _(i):
            for c in range(CHUNKS):
                f_copy(i, c).wait_send()

    @pl.when(s > 0)
    def _():
        @pl.loop(0, blocks)
        def _(i):
            for c in range(CHUNKS):
                b_copy(i, c).wait_send()


def per_device(latents, upstream, proj_in, proj_out, norm_gain):
    stages = lax.axis_size("pipe")
    shards = lax.axis_size("fsdp")
    features = latents.shape[2]
    inner = proj_in.shape[2]
    share = features // shards
    blocks = latents.shape[0] * latents.shape[1] // TOKENS
    lat = latents.reshape(blocks // 2, ROWS, features)
    up = upstream.reshape(blocks // 2, ROWS, features)
    vmem = pl.BlockSpec(memory_space=pltpu.VMEM)
    anywhere = pl.BlockSpec(memory_space=pltpu.HBM)

    def low(*shape):
        return pltpu.VMEM(shape, jnp.bfloat16)

    def high(*shape):
        return pltpu.VMEM(shape, jnp.float32)

    def sems(*shape):
        return pltpu.SemaphoreType.DMA(shape)

    tall, flat = (share, inner), (inner, share)
    grad_in, grad_out = pl.pallas_call(
        functools.partial(relay_kernel, stages, blocks, features),
        out_shape=(
            jax.ShapeDtypeStruct(tall, jnp.bfloat16),
            jax.ShapeDtypeStruct(flat, jnp.bfloat16),
        ),
        in_specs=[anywhere] * 5,
        out_specs=(vmem, vmem),
        scratch_shapes=[
            low(features, inner), low(inner, features), low(inner, features), low(features, inner),
            low(*tall), high(1, share), high(share, 128),
            low(blocks // 2, ROWS, features), *[low(blocks, ROWS, features // 2)] * 4,
            *[high(blocks, TOKENS, inner)] * 3, *[low(2, blocks, ROWS, inner)] * 2,
            low(8, *tall), low(8, *flat), low(8, *tall), low(8, *flat),
            low(2, 3, *tall), low(2, 3, *flat), low(2, 3, *tall), low(2, 3, *flat),
            low(*tall), low(*flat), low(*tall), low(*flat), high(2, *tall), high(2, *flat),
            sems(3), pltpu.SemaphoreType.DMA, *[sems(blocks, CHUNKS)] * 4, sems(4, shards, 2), sems(shards, 2),
            sems(8, 2), sems(8, 2), sems(2, 3, 2), sems(2, 3, 2), sems(2), sems(2),
            pltpu.SemaphoreType.REGULAR,
        ],
        compiler_params=pltpu.CompilerParams(
            collective_id=0, has_side_effects=True, vmem_limit_bytes=VMEM_BYTES
        ),
        name="relay",
    )(lat, up, proj_in[0], proj_out[0], norm_gain)
    return grad_in[None], grad_out[None]


def solution(mesh):
    in_specs = (
        P(None, "fsdp", None),
        P(None, "fsdp", None),
        P("pipe", "fsdp", None),
        P("pipe", None, "fsdp"),
        P("pipe", None),
    )
    out_specs = (P("pipe", "fsdp", None), P("pipe", None, "fsdp"))
    return jax.shard_map(
        per_device, mesh=mesh, in_specs=in_specs, out_specs=out_specs, check_vma=False
    )
```

```python
import functools

import jax
import jax.numpy as jnp
from jax import lax
from jax.experimental import pallas as pl
from jax.experimental.pallas import tpu as pltpu
from jax.sharding import PartitionSpec as P

MESH = pl.DeviceIdType.MESH
epsilon = 1e-06
root_half = 0.7071067811865476
inv_root_tau = 0.3989422804014327
TOKENS = 8
ROWS = 16
CHUNKS = 3
LAG = 2
VMEM_BYTES = 64 * 1024 * 1024 - 65536


def relay_kernel(
    stages, blocks, features,
    lat_ref, up_ref, pin_ref, pout_ref, gain_ref, gin_ref, gout_ref,
    win_ref, wout_ref, win_t, wout_t, own_in, own_gain, gain_s, top,
    h_in, h_out, g_in, g_out, slope_s, pre_s, inv_s, act_s, q_s,
    pair_in, pair_out, pair_in_stage, pair_out_stage,
    ring_in, ring_out, ring_in_stage, ring_out_stage,
    far_in, far_out, far_in_stage, far_out_stage, sum_in, sum_out,
    load_sem, top_sem, f_send, f_recv, b_send, b_recv, ag_send, ag_recv,
    pair_send, pair_recv, ring_send, ring_recv, far_send, far_recv, turn,
):
    s = lax.axis_index("pipe")
    f = lax.axis_index("fsdp")
    fold = features // 2
    wide = fold // CHUNKS
    inner = pin_ref.shape[1]
    share = pin_ref.shape[0]
    after = lax.rem(s + 1, stages)
    before = lax.rem(s + stages - 1, stages)
    half = f // 8
    place = lax.rem(f, 8) // 2
    core = lax.rem(f, 2)

    def index_of(z, x, c):
        return z * 8 + lax.rem(x + 4, 4) * 2 + c

    right = index_of(half, place + 1, core)
    left = index_of(half, place - 1, core)
    pair = index_of(half, place, 1 - core)
    far = index_of(1 - half, place, core)

    def rows_of(j):
        return pl.ds(pl.multiple_of(j * share, 128), share)

    loads = (
        pltpu.make_async_copy(gain_ref.at[:, rows_of(f)], own_gain, load_sem.at[0]),
        pltpu.make_async_copy(pin_ref, own_in, load_sem.at[1]),
        pltpu.make_async_copy(pout_ref, wout_ref.at[:, rows_of(f)], load_sem.at[2]),
    )
    for load in loads:
        load.start()

    barrier = pltpu.get_barrier_semaphore()
    for other in ((before, f), (after, f), (s, right), (s, left), (s, pair), (s, far)):
        pl.semaphore_signal(barrier, inc=1, device_id=other, device_id_type=MESH)

    for load in loads:
        load.wait()
    gain_s[...] = jnp.broadcast_to(own_gain[...], (128, share)).T

    def gains():
        return jnp.concatenate([gain_s[...]] * (inner // 128), axis=1)

    win_ref[rows_of(f), :] = (own_in[...].astype(jnp.float32) * gains()).astype(jnp.bfloat16)
    def columns(c):
        return pl.ds(c * wide, wide)

    def folded(upper, lower):
        return jnp.concatenate([upper, lower], axis=0)

    def load_folded(source, target, land, sem):
        load = pltpu.make_async_copy(source, top, top_sem)
        load.start()
        load.wait()

        @pl.loop(0, blocks // 2)
        def _(i):
            for c in range(CHUNKS):
                low = top[i, :, columns(c)].astype(jnp.float32)
                high = top[i, :, pl.ds(fold + c * wide, wide)].astype(jnp.float32)
                for k in (0, 1):
                    rows = slice(k * TOKENS, (k + 1) * TOKENS)
                    target[2 * i + k, :, columns(c)] = folded(low[rows], high[rows]).astype(jnp.bfloat16)
                    pltpu.make_async_copy(
                        target.at[2 * i + k, :, columns(c)], land.at[2 * i + k, :, columns(c)],
                        sem.at[2 * i + k, c],
                    ).start()

    @pl.when(s == 0)
    def _():
        load_folded(lat_ref, g_out, h_in, f_recv)

    @pl.when(s == stages - 1)
    def _():
        load_folded(up_ref, h_out, g_in, b_recv)

    pl.semaphore_wait(barrier, 6)

    routes = (far, right, left, pair)

    def shard(j, piece):
        return win_ref.at[rows_of(j), :] if piece == 0 else wout_ref.at[:, rows_of(j)]

    def spread(j, piece, route):
        return pltpu.make_async_remote_copy(
            src_ref=shard(j, piece), dst_ref=shard(j, piece),
            send_sem=ag_send.at[route, j, piece], recv_sem=ag_recv.at[j, piece],
            device_id=(s, routes[route]), device_id_type=MESH,
        )

    sent = []

    def share_out(j, piece, *ways):
        for way in ways:
            spread(j, piece, way).start()
            sent.append((j, piece, way))

    def arrived(j, piece):
        spread(j, piece, 3).wait_recv()

    def reach_far(turn):
        @pl.when(lax.rem(s, 4) == turn)
        def _():
            for piece in (0, 1):
                spread(f, piece, 0).start()

    for piece in (0, 1):
        sent.append((f, piece, 0))
    reach_far(0)
    for piece in (0, 1):
        share_out(f, piece, 1, 2)
    for piece in (0, 1):
        share_out(f, piece, 3)

    def f_copy(i, c):
        return pltpu.make_async_remote_copy(
            src_ref=h_out.at[i, :, columns(c)], dst_ref=h_in.at[i, :, columns(c)],
            send_sem=f_send.at[i, c], recv_sem=f_recv.at[i, c],
            device_id=(after, f), device_id_type=MESH,
        )

    def b_copy(i, c):
        return pltpu.make_async_remote_copy(
            src_ref=g_out.at[i, :, columns(c)], dst_ref=g_in.at[i, :, columns(c)],
            send_sem=b_send.at[i, c], recv_sem=b_recv.at[i, c],
            device_id=(before, f), device_id_type=MESH,
        )

    for z in (half, 1 - half):
        mine, on_left, on_right, across = [index_of(z, place + step, core) for step in (0, -1, 1, 2)]
        if z is not half:
            for piece in (0, 1):
                arrived(mine, piece)
                share_out(mine, piece, 1, 2, 3)
        arrived(on_left, 0)
        share_out(on_left, 0, 1, 3)
        if z is half:
            reach_far(1)
        arrived(on_right, 0)
        share_out(on_right, 0, 3)
        arrived(on_right, 1)
        share_out(on_right, 1, 2, 3)
        arrived(on_left, 1)
        share_out(on_left, 1, 3)
        if z is half:
            reach_far(2)
        for piece in (0, 1):
            arrived(across, piece)
            share_out(across, piece, 3)
        if z is half:
            reach_far(3)
    for z in (half, 1 - half):
        for step in (0, -1, 1, 2):
            for piece in (0, 1):
                arrived(index_of(z, place + step, 1 - core), piece)
    def transpose_weights():
        @pl.loop(0, features // 512)
        def _(n):
            cut = pl.ds(pl.multiple_of(n * 512, 512), 512)
            wout_t[cut, :] = wout_ref[:, cut].T
            win_t[:, cut] = win_ref[cut, :].T

    def forward(i):
        low = jnp.zeros((ROWS, inner), jnp.float32)
        high = jnp.zeros((ROWS, inner), jnp.float32)
        square = jnp.zeros((ROWS, 1), jnp.float32)
        for c in range(CHUNKS):
            f_copy(i, c).wait_recv()
            h = h_in[i, :, columns(c)]
            low += jnp.dot(h, win_ref[columns(c), :], preferred_element_type=jnp.float32)
            high += jnp.dot(
                h, win_ref[pl.ds(fold + c * wide, wide), :], preferred_element_type=jnp.float32
            )
            wide_h = h.astype(jnp.float32)
            square += jnp.sum(wide_h * wide_h, axis=-1, keepdims=True)
        square = square[:TOKENS] + square[TOKENS:]
        inverse = lax.rsqrt(square * (1.0 / features) + epsilon)
        pre = (low[:TOKENS] + high[TOKENS:]) * inverse
        cdf = 0.5 * (1.0 + lax.erf(pre * root_half))
        act = pre * cdf

        @pl.when(s < stages - 1)
        def _():
            both = folded(act, act).astype(jnp.bfloat16)
            for c in range(CHUNKS):
                upper = jnp.dot(both, wout_ref[:, columns(c)], preferred_element_type=jnp.float32)
                lower = jnp.dot(
                    both, wout_ref[:, pl.ds(fold + c * wide, wide)],
                    preferred_element_type=jnp.float32,
                )
                h_out[i, :, columns(c)] = (
                    h_in[i, :, columns(c)].astype(jnp.float32)
                    + folded(upper[:TOKENS], lower[TOKENS:])
                ).astype(jnp.bfloat16)
                f_copy(i, c).start()

        blank = jnp.zeros_like(act)
        act_s[0, i] = folded(act, blank).astype(jnp.bfloat16)
        act_s[1, i] = folded(blank, act).astype(jnp.bfloat16)
        pre_s[i] = pre
        slope_s[i] = cdf + pre * jnp.exp(-0.5 * pre * pre) * inv_root_tau
        inv_s[i] = jnp.broadcast_to(inverse, pre.shape)

    def backward(i):
        low = jnp.zeros((ROWS, inner), jnp.float32)
        high = jnp.zeros((ROWS, inner), jnp.float32)
        for c in range(CHUNKS):
            b_copy(i, c).wait_recv()
            g = g_in[i, :, columns(c)]
            low += jnp.dot(g, wout_t[columns(c), :], preferred_element_type=jnp.float32)
            high += jnp.dot(
                g, wout_t[pl.ds(fold + c * wide, wide), :], preferred_element_type=jnp.float32
            )
        grad_pre = (low[:TOKENS] + high[TOKENS:]) * slope_s[i]
        inverse = inv_s[i]
        mean = jnp.sum(grad_pre * pre_s[i], axis=-1, keepdims=True) * (1.0 / features)
        q = grad_pre * inverse
        pull = inverse[:, :1] * inverse[:, :1] * mean

        @pl.when(s > 0)
        def _():
            both = folded(q, q).astype(jnp.bfloat16)
            pulls = folded(pull, pull)
            for c in range(CHUNKS):
                upper = jnp.dot(both, win_t[:, columns(c)], preferred_element_type=jnp.float32)
                lower = jnp.dot(
                    both, win_t[:, pl.ds(fold + c * wide, wide)],
                    preferred_element_type=jnp.float32,
                )
                g_out[i, :, columns(c)] = (
                    g_in[i, :, columns(c)].astype(jnp.float32)
                    + folded(upper[:TOKENS], lower[TOKENS:])
                    - pulls * h_in[i, :, columns(c)].astype(jnp.float32)
                ).astype(jnp.bfloat16)
                b_copy(i, c).start()

        blank = jnp.zeros_like(q)
        q_s[0, i] = folded(q, blank).astype(jnp.bfloat16)
        q_s[1, i] = folded(blank, q).astype(jnp.bfloat16)

    @pl.when(s >= 4)
    def _():
        transpose_weights()

    @pl.loop(0, blocks + LAG * (2 * stages - 2))
    def _(tick):
        @pl.when((s < 4) & (tick == LAG * s + blocks))
        def _():
            transpose_weights()

        ahead = tick - LAG * s
        back = tick - LAG * (2 * stages - 2 - s)

        @pl.when((ahead >= 0) & (ahead < blocks))
        def _():
            @pl.when((s == 0) & (core == 1) & (ahead == 0))
            def _():
                pl.semaphore_wait(turn, 1)

            forward(ahead)

            @pl.when((s == 0) & (core == 0) & (ahead == 0))
            def _():
                pl.semaphore_signal(turn, inc=1, device_id=(s, pair), device_id_type=MESH)

        @pl.when((back >= 0) & (back < blocks))
        def _():
            backward(back)

    rows = blocks * ROWS
    over_rows = (((0,), (0,)), ((), ()))

    def cut_of(j):
        return pl.ds(pl.multiple_of(lax.rem(j, 8) * share, 128), share)

    def part_in(j):
        h = h_in[:, :, cut_of(j)].reshape(rows, share)
        q = q_s[j // 8].reshape(rows, inner)
        return lax.dot_general(h, q, over_rows, preferred_element_type=jnp.float32)

    def part_out(j):
        g = g_in[:, :, cut_of(j)].reshape(rows, share)
        act = act_s[j // 8].reshape(rows, inner)
        return lax.dot_general(act, g, over_rows, preferred_element_type=jnp.float32)

    def remote(src, dst, send, recv, route):
        return pltpu.make_async_remote_copy(
            src_ref=src, dst_ref=dst, send_sem=send, recv_sem=recv,
            device_id=(s, routes[route]), device_id_type=MESH,
        )

    def pair_copy(m, piece):
        stage, land = ((pair_in_stage, pair_in), (pair_out_stage, pair_out))[piece]
        return remote(stage.at[m], land.at[m], pair_send.at[m, piece], pair_recv.at[m, piece], 3)

    def ring_copy(h, slot, piece):
        stage, land = ((ring_in_stage, ring_in), (ring_out_stage, ring_out))[piece]
        way = 1 if (slot == 2) == (piece == 1) else 2
        return remote(
            stage.at[h, slot], land.at[h, slot],
            ring_send.at[h, slot, piece], ring_recv.at[h, slot, piece], way,
        )

    def far_copy(piece):
        stage, land = ((far_in_stage, far_in), (far_out_stage, far_out))[piece]
        return remote(stage, land, far_send.at[piece], far_recv.at[piece], 0)

    steps = (2, 1, -1, 0)
    halves = (1 - half, half)
    def pair_share(h, *turns):
        for k in turns:
            m = h * 4 + k
            j = index_of(halves[h], place + steps[k], 1 - core)
            pair_in_stage[m] = part_in(j).astype(jnp.bfloat16)
            pair_copy(m, 0).start()
            pair_out_stage[m] = part_out(j).astype(jnp.bfloat16)
            pair_copy(m, 1).start()

    def both_in(h, k):
        pair_copy(h * 4 + k, 0).wait_recv()
        j = index_of(halves[h], place + steps[k], core)
        return part_in(j) + pair_in[h * 4 + k].astype(jnp.float32)

    def both_out(h, k):
        pair_copy(h * 4 + k, 1).wait_recv()
        j = index_of(halves[h], place + steps[k], core)
        return part_out(j) + pair_out[h * 4 + k].astype(jnp.float32)

    def start_ring(h):
        ring_in_stage[h, 0] = both_in(h, 0).astype(jnp.bfloat16)
        ring_copy(h, 0, 0).start()
        ring_out_stage[h, 0] = both_out(h, 0).astype(jnp.bfloat16)
        ring_copy(h, 0, 1).start()

    def open_ring(h):
        ring_out_stage[h, 2] = both_out(h, 1).astype(jnp.bfloat16)
        ring_copy(h, 2, 1).start()
        ring_in_stage[h, 2] = both_in(h, 2).astype(jnp.bfloat16)
        ring_copy(h, 2, 0).start()
        sum_in[h] = both_in(h, 3)
        sum_out[h] = both_out(h, 3)

    def relay_ring(h):
        own = both_in(h, 1)
        ring_copy(h, 0, 0).wait_recv()
        ring_in_stage[h, 1] = (own + ring_in[h, 0].astype(jnp.float32)).astype(jnp.bfloat16)
        ring_copy(h, 1, 0).start()
        own = both_out(h, 2)
        ring_copy(h, 0, 1).wait_recv()
        ring_out_stage[h, 1] = (own + ring_out[h, 0].astype(jnp.float32)).astype(jnp.bfloat16)
        ring_copy(h, 1, 1).start()

    def total(h, piece):
        kept, land = ((sum_in, ring_in), (sum_out, ring_out))[piece]
        for slot in (2, 1):
            ring_copy(h, slot, piece).wait_recv()
        return kept[h] + land[h, 1].astype(jnp.float32) + land[h, 2].astype(jnp.float32)

    pair_share(0, 0, 1)
    start_ring(0)
    pair_share(0, 2, 3)
    open_ring(0)
    pair_share(1, 0, 1, 2, 3)
    relay_ring(0)
    start_ring(1)
    open_ring(1)
    far_in_stage[...] = total(0, 0).astype(jnp.bfloat16)
    far_copy(0).start()
    far_out_stage[...] = total(0, 1).astype(jnp.bfloat16)
    far_copy(1).start()
    relay_ring(1)
    own = total(1, 0)
    far_copy(0).wait_recv()
    gin_ref[...] = ((own + far_in[...].astype(jnp.float32)) * gains()).astype(jnp.bfloat16)
    own = total(1, 1)
    far_copy(1).wait_recv()
    gout_ref[...] = (own + far_out[...].astype(jnp.float32)).astype(jnp.bfloat16)

    for j, piece, way in sent:
        spread(j, piece, way).wait_send()
    for piece in (0, 1):
        far_copy(piece).wait_send()
        for m in range(8):
            pair_copy(m, piece).wait_send()
        for h in (0, 1):
            for slot in range(3):
                ring_copy(h, slot, piece).wait_send()

    @pl.when(s < stages - 1)
    def _():
        @pl.loop(0, blocks)
        def _(i):
            for c in range(CHUNKS):
                f_copy(i, c).wait_send()

    @pl.when(s > 0)
    def _():
        @pl.loop(0, blocks)
        def _(i):
            for c in range(CHUNKS):
                b_copy(i, c).wait_send()


def per_device(latents, upstream, proj_in, proj_out, norm_gain):
    stages = lax.axis_size("pipe")
    shards = lax.axis_size("fsdp")
    features = latents.shape[2]
    inner = proj_in.shape[2]
    share = features // shards
    blocks = latents.shape[0] * latents.shape[1] // TOKENS
    lat = latents.reshape(blocks // 2, ROWS, features)
    up = upstream.reshape(blocks // 2, ROWS, features)
    vmem = pl.BlockSpec(memory_space=pltpu.VMEM)
    anywhere = pl.BlockSpec(memory_space=pltpu.HBM)

    def low(*shape):
        return pltpu.VMEM(shape, jnp.bfloat16)

    def high(*shape):
        return pltpu.VMEM(shape, jnp.float32)

    def sems(*shape):
        return pltpu.SemaphoreType.DMA(shape)

    tall, flat = (share, inner), (inner, share)
    grad_in, grad_out = pl.pallas_call(
        functools.partial(relay_kernel, stages, blocks, features),
        out_shape=(
            jax.ShapeDtypeStruct(tall, jnp.bfloat16),
            jax.ShapeDtypeStruct(flat, jnp.bfloat16),
        ),
        in_specs=[anywhere] * 5,
        out_specs=(vmem, vmem),
        scratch_shapes=[
            low(features, inner), low(inner, features), low(inner, features), low(features, inner),
            low(*tall), high(1, share), high(share, 128),
            low(blocks // 2, ROWS, features), *[low(blocks, ROWS, features // 2)] * 4,
            *[high(blocks, TOKENS, inner)] * 3, *[low(2, blocks, ROWS, inner)] * 2,
            low(8, *tall), low(8, *flat), low(8, *tall), low(8, *flat),
            low(2, 3, *tall), low(2, 3, *flat), low(2, 3, *tall), low(2, 3, *flat),
            low(*tall), low(*flat), low(*tall), low(*flat), high(2, *tall), high(2, *flat),
            sems(3), pltpu.SemaphoreType.DMA, *[sems(blocks, CHUNKS)] * 4, sems(4, shards, 2), sems(shards, 2),
            sems(8, 2), sems(8, 2), sems(2, 3, 2), sems(2, 3, 2), sems(2), sems(2),
            pltpu.SemaphoreType.REGULAR,
        ],
        compiler_params=pltpu.CompilerParams(
            collective_id=0, has_side_effects=True, vmem_limit_bytes=VMEM_BYTES
        ),
        name="relay",
    )(lat, up, proj_in[0], proj_out[0], norm_gain)
    return grad_in[None], grad_out[None]


def solution(mesh):
    in_specs = (
        P(None, "fsdp", None),
        P(None, "fsdp", None),
        P("pipe", "fsdp", None),
        P("pipe", None, "fsdp"),
        P("pipe", None),
    )
    out_specs = (P("pipe", "fsdp", None), P("pipe", None, "fsdp"))
    return jax.shard_map(
        per_device, mesh=mesh, in_specs=in_specs, out_specs=out_specs, check_vma=False
    )
```

```python
import functools

import jax
import jax.numpy as jnp
from jax import lax
from jax.experimental import pallas as pl
from jax.experimental.pallas import tpu as pltpu
from jax.sharding import PartitionSpec as P

MESH = pl.DeviceIdType.MESH
epsilon = 1e-06
root_half = 0.7071067811865476
inv_root_tau = 0.3989422804014327
TOKENS = 8
ROWS = 16
CHUNKS = 3
LAG = 2
VMEM_BYTES = 64 * 1024 * 1024 - 65536


def relay_kernel(
    stages, blocks, features,
    lat_ref, up_ref, pin_ref, pout_ref, gain_ref, gin_ref, gout_ref,
    win_ref, wout_ref, win_t, wout_t, own_in, own_gain, gain_s, top,
    h_in, h_out, g_in, g_out, slope_s, pre_s, inv_s, act_s, q_s,
    pair_in, pair_out, pair_in_stage, pair_out_stage,
    ring_in, ring_out, ring_in_stage, ring_out_stage,
    far_in, far_out, far_in_stage, far_out_stage, sum_in, sum_out,
    load_sem, top_sem, f_send, f_recv, b_send, b_recv, ag_send, ag_recv,
    pair_send, pair_recv, ring_send, ring_recv, far_send, far_recv, turn,
):
    s = lax.axis_index("pipe")
    f = lax.axis_index("fsdp")
    fold = features // 2
    wide = fold // CHUNKS
    inner = pin_ref.shape[1]
    share = pin_ref.shape[0]
    after = lax.rem(s + 1, stages)
    before = lax.rem(s + stages - 1, stages)
    half = f // 8
    place = lax.rem(f, 8) // 2
    core = lax.rem(f, 2)

    def index_of(z, x, c):
        return z * 8 + lax.rem(x + 4, 4) * 2 + c

    right = index_of(half, place + 1, core)
    left = index_of(half, place - 1, core)
    pair = index_of(half, place, 1 - core)
    far = index_of(1 - half, place, core)

    def rows_of(j):
        return pl.ds(pl.multiple_of(j * share, 128), share)

    loads = (
        pltpu.make_async_copy(gain_ref.at[:, rows_of(f)], own_gain, load_sem.at[0]),
        pltpu.make_async_copy(pin_ref, own_in, load_sem.at[1]),
        pltpu.make_async_copy(pout_ref, wout_ref.at[:, rows_of(f)], load_sem.at[2]),
    )
    for load in loads:
        load.start()

    barrier = pltpu.get_barrier_semaphore()
    for other in ((before, f), (after, f), (s, right), (s, left), (s, pair), (s, far)):
        pl.semaphore_signal(barrier, inc=1, device_id=other, device_id_type=MESH)

    for load in loads:
        load.wait()
    gain_s[...] = jnp.broadcast_to(own_gain[...], (128, share)).T

    def gains():
        return jnp.concatenate([gain_s[...]] * (inner // 128), axis=1)

    win_ref[rows_of(f), :] = (own_in[...].astype(jnp.float32) * gains()).astype(jnp.bfloat16)
    def columns(c):
        return pl.ds(c * wide, wide)

    def folded(upper, lower):
        return jnp.concatenate([upper, lower], axis=0)

    def load_folded(source, target, land, sem):
        load = pltpu.make_async_copy(source, top, top_sem)
        load.start()
        load.wait()

        @pl.loop(0, blocks // 2)
        def _(i):
            for c in range(CHUNKS):
                low = top[i, :, columns(c)].astype(jnp.float32)
                high = top[i, :, pl.ds(fold + c * wide, wide)].astype(jnp.float32)
                for k in (0, 1):
                    rows = slice(k * TOKENS, (k + 1) * TOKENS)
                    target[2 * i + k, :, columns(c)] = folded(low[rows], high[rows]).astype(jnp.bfloat16)
                    pltpu.make_async_copy(
                        target.at[2 * i + k, :, columns(c)], land.at[2 * i + k, :, columns(c)],
                        sem.at[2 * i + k, c],
                    ).start()

    @pl.when(s == 0)
    def _():
        load_folded(lat_ref, g_out, h_in, f_recv)

    @pl.when(s == stages - 1)
    def _():
        load_folded(up_ref, h_out, g_in, b_recv)

    pl.semaphore_wait(barrier, 6)

    routes = (far, right, left, pair)

    def shard(j, piece):
        return win_ref.at[rows_of(j), :] if piece == 0 else wout_ref.at[:, rows_of(j)]

    def spread(j, piece, route):
        return pltpu.make_async_remote_copy(
            src_ref=shard(j, piece), dst_ref=shard(j, piece),
            send_sem=ag_send.at[route, j, piece], recv_sem=ag_recv.at[j, piece],
            device_id=(s, routes[route]), device_id_type=MESH,
        )

    sent = []

    def share_out(j, piece, *ways):
        for way in ways:
            spread(j, piece, way).start()
            sent.append((j, piece, way))

    def arrived(j, piece):
        spread(j, piece, 3).wait_recv()

    def reach_far(turn):
        @pl.when(lax.rem(s, 4) == turn)
        def _():
            for piece in (0, 1):
                spread(f, piece, 0).start()

    for piece in (0, 1):
        sent.append((f, piece, 0))
    reach_far(0)
    for piece in (0, 1):
        share_out(f, piece, 1, 2)
    for piece in (0, 1):
        share_out(f, piece, 3)

    def f_copy(i, c):
        return pltpu.make_async_remote_copy(
            src_ref=h_out.at[i, :, columns(c)], dst_ref=h_in.at[i, :, columns(c)],
            send_sem=f_send.at[i, c], recv_sem=f_recv.at[i, c],
            device_id=(after, f), device_id_type=MESH,
        )

    def b_copy(i, c):
        return pltpu.make_async_remote_copy(
            src_ref=g_out.at[i, :, columns(c)], dst_ref=g_in.at[i, :, columns(c)],
            send_sem=b_send.at[i, c], recv_sem=b_recv.at[i, c],
            device_id=(before, f), device_id_type=MESH,
        )

    for z in (half, 1 - half):
        mine, on_left, on_right, across = [index_of(z, place + step, core) for step in (0, -1, 1, 2)]
        if z is not half:
            for piece in (0, 1):
                arrived(mine, piece)
                share_out(mine, piece, 1, 2, 3)
        arrived(on_left, 0)
        share_out(on_left, 0, 1, 3)
        if z is half:
            reach_far(1)
        arrived(on_right, 0)
        share_out(on_right, 0, 3)
        arrived(on_right, 1)
        share_out(on_right, 1, 2, 3)
        arrived(on_left, 1)
        share_out(on_left, 1, 3)
        if z is half:
            reach_far(2)
        for piece in (0, 1):
            arrived(across, piece)
            share_out(across, piece, 3)
        if z is half:
            reach_far(3)
    for z in (half, 1 - half):
        for step in (0, -1, 1, 2):
            for piece in (0, 1):
                arrived(index_of(z, place + step, 1 - core), piece)
    def transpose_weights():
        @pl.loop(0, features // 512)
        def _(n):
            cut = pl.ds(pl.multiple_of(n * 512, 512), 512)
            wout_t[cut, :] = wout_ref[:, cut].T
            win_t[:, cut] = win_ref[cut, :].T

    def forward(i):
        low = jnp.zeros((ROWS, inner), jnp.float32)
        high = jnp.zeros((ROWS, inner), jnp.float32)
        square = jnp.zeros((ROWS, 1), jnp.float32)
        for c in range(CHUNKS):
            f_copy(i, c).wait_recv()
            h = h_in[i, :, columns(c)]
            low += jnp.dot(h, win_ref[columns(c), :], preferred_element_type=jnp.float32)
            high += jnp.dot(
                h, win_ref[pl.ds(fold + c * wide, wide), :], preferred_element_type=jnp.float32
            )
            wide_h = h.astype(jnp.float32)
            square += jnp.sum(wide_h * wide_h, axis=-1, keepdims=True)
        square = square[:TOKENS] + square[TOKENS:]
        inverse = lax.rsqrt(square * (1.0 / features) + epsilon)
        pre = (low[:TOKENS] + high[TOKENS:]) * inverse
        cdf = 0.5 * (1.0 + lax.erf(pre * root_half))
        act = pre * cdf

        @pl.when(s < stages - 1)
        def _():
            both = folded(act, act).astype(jnp.bfloat16)
            for c in range(CHUNKS):
                upper = jnp.dot(both, wout_ref[:, columns(c)], preferred_element_type=jnp.float32)
                lower = jnp.dot(
                    both, wout_ref[:, pl.ds(fold + c * wide, wide)],
                    preferred_element_type=jnp.float32,
                )
                h_out[i, :, columns(c)] = (
                    h_in[i, :, columns(c)].astype(jnp.float32)
                    + folded(upper[:TOKENS], lower[TOKENS:])
                ).astype(jnp.bfloat16)
                f_copy(i, c).start()

        blank = jnp.zeros_like(act)
        act_s[0, i] = folded(act, blank).astype(jnp.bfloat16)
        act_s[1, i] = folded(blank, act).astype(jnp.bfloat16)
        pre_s[i] = pre
        slope_s[i] = cdf + pre * jnp.exp(-0.5 * pre * pre) * inv_root_tau
        inv_s[i] = jnp.broadcast_to(inverse, pre.shape)

    def backward(i):
        low = jnp.zeros((ROWS, inner), jnp.float32)
        high = jnp.zeros((ROWS, inner), jnp.float32)
        for c in range(CHUNKS):
            b_copy(i, c).wait_recv()
            g = g_in[i, :, columns(c)]
            low += jnp.dot(g, wout_t[columns(c), :], preferred_element_type=jnp.float32)
            high += jnp.dot(
                g, wout_t[pl.ds(fold + c * wide, wide), :], preferred_element_type=jnp.float32
            )
        grad_pre = (low[:TOKENS] + high[TOKENS:]) * slope_s[i]
        inverse = inv_s[i]
        mean = jnp.sum(grad_pre * pre_s[i], axis=-1, keepdims=True) * (1.0 / features)
        q = grad_pre * inverse
        pull = inverse[:, :1] * inverse[:, :1] * mean

        @pl.when(s > 0)
        def _():
            both = folded(q, q).astype(jnp.bfloat16)
            pulls = folded(pull, pull)
            for c in range(CHUNKS):
                upper = jnp.dot(both, win_t[:, columns(c)], preferred_element_type=jnp.float32)
                lower = jnp.dot(
                    both, win_t[:, pl.ds(fold + c * wide, wide)],
                    preferred_element_type=jnp.float32,
                )
                g_out[i, :, columns(c)] = (
                    g_in[i, :, columns(c)].astype(jnp.float32)
                    + folded(upper[:TOKENS], lower[TOKENS:])
                    - pulls * h_in[i, :, columns(c)].astype(jnp.float32)
                ).astype(jnp.bfloat16)
                b_copy(i, c).start()

        blank = jnp.zeros_like(q)
        q_s[0, i] = folded(q, blank).astype(jnp.bfloat16)
        q_s[1, i] = folded(blank, q).astype(jnp.bfloat16)

    @pl.when(s >= 4)
    def _():
        transpose_weights()

    @pl.loop(0, blocks + LAG * (2 * stages - 2))
    def _(tick):
        @pl.when((s < 4) & (tick == LAG * s + blocks))
        def _():
            transpose_weights()

        ahead = tick - LAG * s
        back = tick - LAG * (2 * stages - 2 - s)

        @pl.when((ahead >= 0) & (ahead < blocks))
        def _():
            @pl.when((s == 0) & (core == 1) & (ahead == 0))
            def _():
                pl.semaphore_wait(turn, 1)

            forward(ahead)

            @pl.when((s == 0) & (core == 0) & (ahead == 0))
            def _():
                pl.semaphore_signal(turn, inc=1, device_id=(s, pair), device_id_type=MESH)

        @pl.when((back >= 0) & (back < blocks))
        def _():
            backward(back)

    rows = blocks * ROWS
    over_rows = (((0,), (0,)), ((), ()))

    def cut_of(j):
        return pl.ds(pl.multiple_of(lax.rem(j, 8) * share, 128), share)

    def part_in(j):
        h = h_in[:, :, cut_of(j)].reshape(rows, share)
        q = q_s[j // 8].reshape(rows, inner)
        return lax.dot_general(h, q, over_rows, preferred_element_type=jnp.float32)

    def part_out(j):
        g = g_in[:, :, cut_of(j)].reshape(rows, share)
        act = act_s[j // 8].reshape(rows, inner)
        return lax.dot_general(act, g, over_rows, preferred_element_type=jnp.float32)

    def remote(src, dst, send, recv, route):
        return pltpu.make_async_remote_copy(
            src_ref=src, dst_ref=dst, send_sem=send, recv_sem=recv,
            device_id=(s, routes[route]), device_id_type=MESH,
        )

    def pair_copy(m, piece):
        stage, land = ((pair_in_stage, pair_in), (pair_out_stage, pair_out))[piece]
        return remote(stage.at[m], land.at[m], pair_send.at[m, piece], pair_recv.at[m, piece], 3)

    def ring_copy(h, slot, piece):
        stage, land = ((ring_in_stage, ring_in), (ring_out_stage, ring_out))[piece]
        way = 1 if (slot == 2) == (piece == 1) else 2
        return remote(
            stage.at[h, slot], land.at[h, slot],
            ring_send.at[h, slot, piece], ring_recv.at[h, slot, piece], way,
        )

    def far_copy(piece):
        stage, land = ((far_in_stage, far_in), (far_out_stage, far_out))[piece]
        return remote(stage, land, far_send.at[piece], far_recv.at[piece], 0)

    steps = (2, 1, -1, 0)
    halves = (1 - half, half)
    def pair_share(h):
        for k, step in enumerate(steps):
            m = h * 4 + k
            j = index_of(halves[h], place + step, 1 - core)
            pair_in_stage[m] = part_in(j).astype(jnp.bfloat16)
            pair_copy(m, 0).start()
            pair_out_stage[m] = part_out(j).astype(jnp.bfloat16)
            pair_copy(m, 1).start()

    def both_in(h, k):
        pair_copy(h * 4 + k, 0).wait_recv()
        j = index_of(halves[h], place + steps[k], core)
        return part_in(j) + pair_in[h * 4 + k].astype(jnp.float32)

    def both_out(h, k):
        pair_copy(h * 4 + k, 1).wait_recv()
        j = index_of(halves[h], place + steps[k], core)
        return part_out(j) + pair_out[h * 4 + k].astype(jnp.float32)

    def open_ring(h):
        ring_in_stage[h, 0] = both_in(h, 0).astype(jnp.bfloat16)
        ring_copy(h, 0, 0).start()
        ring_out_stage[h, 0] = both_out(h, 0).astype(jnp.bfloat16)
        ring_copy(h, 0, 1).start()
        ring_out_stage[h, 2] = both_out(h, 1).astype(jnp.bfloat16)
        ring_copy(h, 2, 1).start()
        ring_in_stage[h, 2] = both_in(h, 2).astype(jnp.bfloat16)
        ring_copy(h, 2, 0).start()
        sum_in[h] = both_in(h, 3)
        sum_out[h] = both_out(h, 3)

    def relay_ring(h):
        own = both_in(h, 1)
        ring_copy(h, 0, 0).wait_recv()
        ring_in_stage[h, 1] = (own + ring_in[h, 0].astype(jnp.float32)).astype(jnp.bfloat16)
        ring_copy(h, 1, 0).start()
        own = both_out(h, 2)
        ring_copy(h, 0, 1).wait_recv()
        ring_out_stage[h, 1] = (own + ring_out[h, 0].astype(jnp.float32)).astype(jnp.bfloat16)
        ring_copy(h, 1, 1).start()

    def total(h, piece):
        kept, land = ((sum_in, ring_in), (sum_out, ring_out))[piece]
        for slot in (2, 1):
            ring_copy(h, slot, piece).wait_recv()
        return kept[h] + land[h, 1].astype(jnp.float32) + land[h, 2].astype(jnp.float32)

    pair_share(0)
    open_ring(0)
    pair_share(1)
    for j, piece, way in sent:
        spread(j, piece, way).wait_send()

    @pl.when(s < stages - 1)
    def _():
        @pl.loop(0, blocks)
        def _(i):
            for c in range(CHUNKS):
                f_copy(i, c).wait_send()

    @pl.when(s > 0)
    def _():
        @pl.loop(0, blocks)
        def _(i):
            for c in range(CHUNKS):
                b_copy(i, c).wait_send()

    relay_ring(0)
    open_ring(1)
    far_in_stage[...] = total(0, 0).astype(jnp.bfloat16)
    far_copy(0).start()
    far_out_stage[...] = total(0, 1).astype(jnp.bfloat16)
    far_copy(1).start()
    relay_ring(1)
    own = total(1, 0)
    far_copy(0).wait_recv()
    gin_ref[...] = ((own + far_in[...].astype(jnp.float32)) * gains()).astype(jnp.bfloat16)
    own = total(1, 1)
    far_copy(1).wait_recv()
    gout_ref[...] = (own + far_out[...].astype(jnp.float32)).astype(jnp.bfloat16)

    for piece in (0, 1):
        far_copy(piece).wait_send()
        for m in range(8):
            pair_copy(m, piece).wait_send()
        for h in (0, 1):
            for slot in range(3):
                ring_copy(h, slot, piece).wait_send()


def per_device(latents, upstream, proj_in, proj_out, norm_gain):
    stages = lax.axis_size("pipe")
    shards = lax.axis_size("fsdp")
    features = latents.shape[2]
    inner = proj_in.shape[2]
    share = features // shards
    blocks = latents.shape[0] * latents.shape[1] // TOKENS
    lat = latents.reshape(blocks // 2, ROWS, features)
    up = upstream.reshape(blocks // 2, ROWS, features)
    vmem = pl.BlockSpec(memory_space=pltpu.VMEM)
    anywhere = pl.BlockSpec(memory_space=pltpu.HBM)

    def low(*shape):
        return pltpu.VMEM(shape, jnp.bfloat16)

    def high(*shape):
        return pltpu.VMEM(shape, jnp.float32)

    def sems(*shape):
        return pltpu.SemaphoreType.DMA(shape)

    tall, flat = (share, inner), (inner, share)
    grad_in, grad_out = pl.pallas_call(
        functools.partial(relay_kernel, stages, blocks, features),
        out_shape=(
            jax.ShapeDtypeStruct(tall, jnp.bfloat16),
            jax.ShapeDtypeStruct(flat, jnp.bfloat16),
        ),
        in_specs=[anywhere] * 5,
        out_specs=(vmem, vmem),
        scratch_shapes=[
            low(features, inner), low(inner, features), low(inner, features), low(features, inner),
            low(*tall), high(1, share), high(share, 128),
            low(blocks // 2, ROWS, features), *[low(blocks, ROWS, features // 2)] * 4,
            *[high(blocks, TOKENS, inner)] * 3, *[low(2, blocks, ROWS, inner)] * 2,
            low(8, *tall), low(8, *flat), low(8, *tall), low(8, *flat),
            low(2, 3, *tall), low(2, 3, *flat), low(2, 3, *tall), low(2, 3, *flat),
            low(*tall), low(*flat), low(*tall), low(*flat), high(2, *tall), high(2, *flat),
            sems(3), pltpu.SemaphoreType.DMA, *[sems(blocks, CHUNKS)] * 4, sems(4, shards, 2), sems(shards, 2),
            sems(8, 2), sems(8, 2), sems(2, 3, 2), sems(2, 3, 2), sems(2), sems(2),
            pltpu.SemaphoreType.REGULAR,
        ],
        compiler_params=pltpu.CompilerParams(
            collective_id=0, has_side_effects=True, vmem_limit_bytes=VMEM_BYTES
        ),
        name="relay",
    )(lat, up, proj_in[0], proj_out[0], norm_gain)
    return grad_in[None], grad_out[None]


def solution(mesh):
    in_specs = (
        P(None, "fsdp", None),
        P(None, "fsdp", None),
        P("pipe", "fsdp", None),
        P("pipe", None, "fsdp"),
        P("pipe", None),
    )
    out_specs = (P("pipe", "fsdp", None), P("pipe", None, "fsdp"))
    return jax.shard_map(
        per_device, mesh=mesh, in_specs=in_specs, out_specs=out_specs, check_vma=False
    )
```
